256 devices in a mesh: batch: 16 (over x, z_lo), centre: 16 (over y, z_hi, core).
Axes of the slice: x: 4, y: 4, z: 8 (z_hi: 2, z_lo: 4; z = z_hi * 4 + z_lo), core: 2. Of those that a mesh axis runs over, the one named last changes fastest.
Arguments:
- batch_features: float32 [8192, 768], P(('batch', 'centre')), may hold values from -1 to 1
- centre_features: float32 [8192, 768], P(('centre', 'batch')), may hold values from -1 to 1
- targets: float32 [8192, 512], P(('batch', 'centre')), may hold values from -6 to 6
- weights: float32 [8192, 512], P(('centre', 'batch')), may hold values from -0.5 to 0.5
Outputs:
- residual: float32 [8192, 512], P(('batch', 'centre'))
- update: float32 [8192, 512], P(('centre', 'batch'))
The draws below stay inside these ranges and needn't reach their ends.
All inputs are finite; a program needn't handle non-finite values.
Results may differ from the reference program's by a relative error of at most 0.000061.
Values sent between devices are 32-bit elements; how exact they have to be, the bound alone decides.
No kernel may reach another device: no remote copies, remote signals or barrier semaphores. Data moves between devices by JAX's collectives and lax.ppermute only.
A program may use at most 64 MiB of HBM per device.

```python
import math
import jax
import jax.numpy as jnp
from jax import lax

D = 768
OUTW = 512
B_DEV = 512
C_DEV = 512
B = 8192
C = 8192
N_BATCH = 16
N_CENTRE = 16


cluster_count = 64


latent_rank = 32


def feature_rows(key, salt, count):
    shared = jax.random.fold_in(key, 7)
    key_means, key_basis, key_spread = jax.random.split(shared, 3)
    key_pick, key_latent, key_noise = jax.random.split(jax.random.fold_in(key, salt), 3)
    means = jax.random.normal(key_means, (cluster_count, D), jnp.float32)
    means = means / jnp.sqrt(jnp.sum(means * means, axis=1, keepdims=True))
    basis = jax.random.normal(key_basis, (latent_rank, D), jnp.float32) * math.sqrt(0.6 / (latent_rank * D))
    positions = jnp.arange(count, dtype=jnp.int32)
    upper = cluster_count - 48 * positions // count
    picks = jax.random.randint(key_pick, (count,), 0, upper).astype(jnp.int32)
    coeffs = jax.random.normal(key_latent, (count, latent_rank), jnp.float32)
    latent = jnp.dot(coeffs, basis, precision=lax.Precision.HIGHEST, preferred_element_type=jnp.float32)
    spread = jnp.exp(jax.random.uniform(key_spread, (cluster_count, 1), jnp.float32, math.log(0.15), math.log(1.5)))
    noise = jax.random.normal(key_noise, (count, D), jnp.float32) * math.sqrt(0.25 / D)
    raw = means[picks] + spread[picks] * (latent + noise)
    return raw / jnp.sqrt(jnp.sum(raw * raw, axis=1, keepdims=True))


def draw_batch_features(key, part):
    return feature_rows(key, 11, B)


def draw_centre_features(key, part):
    return feature_rows(key, 23, C)


def shard_levels(own_key, shape, cuts, low, top_value):
    loudness = 1.0
    for dim, shards_of in cuts:
        heights = jax.random.uniform(jax.random.fold_in(jax.random.fold_in(own_key, 6), dim), (shards_of,), jnp.float32, low / len(cuts), top_value / len(cuts))
        loudness = loudness * jnp.repeat(jnp.exp(heights), shape[dim] // shards_of).reshape((-1,) + (1,) * (len(shape) - 1 - dim))
    return loudness


def normal_values(own_key, shape, deviation, bound, cuts=(), held_as=jnp.bfloat16):
    result = deviation * jax.random.normal(own_key, shape, jnp.float32)
    if cuts:
        result = result * shard_levels(own_key, shape, cuts, -0.22, 0.18)
    return jnp.clip(result, -bound, bound).astype(held_as)


def setup_inputs(seed: int = 0) -> dict:
    arg_keys = jax.random.split(jax.random.key(seed), 5)
    batch_features = draw_batch_features(jax.random.fold_in(arg_keys[4], 71), 0)
    centre_features = draw_centre_features(jax.random.fold_in(arg_keys[4], 71), 0)
    targets = normal_values(arg_keys[2], (B, OUTW), 1.0, 6.0, ((0, 256),), jnp.float32)
    weights = normal_values(arg_keys[3], (C, OUTW), (max(C // 64, 1)) ** -0.5, 0.5, ((0, 256),), jnp.float32)
    return {"batch_features": batch_features, "centre_features": centre_features, "targets": targets, "weights": weights}


length_scale = 0.5
softening = 0.01

def kernel_matrix(left_rows, right_rows):
    left_norms = lax.optimization_barrier(jnp.sum(left_rows * left_rows, axis=1))
    right_norms = lax.optimization_barrier(jnp.sum(right_rows * right_rows, axis=1))
    inner = lax.dot_general(left_rows, right_rows, (((1,), (1,)), ((), ())), precision=lax.Precision.HIGHEST, preferred_element_type=jnp.float32)
    squared = left_norms[:, None] + right_norms[None, :] - 2.0 * inner
    return jnp.exp(-jnp.sqrt(squared + softening) / length_scale)

def reference(batch_features, centre_features, targets, weights):
    batch_blocks = batch_features.reshape(N_BATCH, B_DEV, D)
    centre_blocks = centre_features.reshape(N_CENTRE, C_DEV, D)

    def predict(block):
        return jnp.dot(kernel_matrix(block, centre_features), weights, precision=lax.Precision.HIGHEST, preferred_element_type=jnp.float32)
    pred = lax.map(predict, batch_blocks).reshape(B, OUTW)
    residual = pred - targets

    def project(block):
        return jnp.dot(kernel_matrix(block, batch_features), residual, precision=lax.Precision.HIGHEST, preferred_element_type=jnp.float32)
    gradient = lax.map(project, centre_blocks).reshape(C, OUTW)

    def correct(block):
        kernel_block = kernel_matrix(block, centre_features)
        return (lax.optimization_barrier(jnp.sum(kernel_block, axis=1)), jnp.dot(kernel_block, gradient, precision=lax.Precision.HIGHEST, preferred_element_type=jnp.float32))
    row_sums, product = lax.map(correct, centre_blocks)
    row_sums = row_sums.reshape(C)
    product = product.reshape(C, OUTW)
    step_size = 1.0 / jnp.max(row_sums)
    theta = 2.0 * step_size * gradient - step_size * step_size * product
    update = theta * (C / math.sqrt(B))
    return (residual, update)
```

```python
import math

import jax
import jax.numpy as jnp
from jax import lax
from jax.sharding import Mesh
from jax.sharding import PartitionSpec as P

length_scale = 0.5
softening = 0.01
plane = ("x", "y")
ring = ("z_hi", "z_lo")
swap = [(0, 1), (1, 0)]


def gather(value, axis):
    copies = jnp.broadcast_to(value[None], (lax.axis_size(axis),) + value.shape)
    return lax.all_to_all(copies, axis, 0, 0)


def exchange(parts, axis):
    return jnp.sum(lax.all_to_all(parts, axis, 0, 0), axis=0)


def both_cores(value):
    return jnp.stack([value, lax.ppermute(value, "core", swap)])


def to_columns(rows):
    core = lax.axis_index("core")
    half = rows.shape[1] // 2
    first, second = rows[:, :half], rows[:, half:]
    own = jnp.where(core == 0, first, second)
    other = jnp.where(core == 0, second, first)
    return jnp.stack([own, lax.ppermute(other, "core", swap)])


def to_rows(columns):
    core = lax.axis_index("core")
    own, other = columns[0], lax.ppermute(columns[1], "core", swap)
    first = jnp.where(core == 0, own, other)
    second = jnp.where(core == 0, other, own)
    return jnp.concatenate([first, second], axis=1)


def dot(left, right, contract, precision=lax.Precision.HIGHEST):
    return lax.dot_general(
        left, right, (contract, ((), ())), precision=precision, preferred_element_type=jnp.float32
    )


def kernel_matrix(left_rows, right_rows):
    left_norms = jnp.sum(left_rows * left_rows, axis=1)
    right_norms = jnp.sum(right_rows * right_rows, axis=1)
    inner = dot(left_rows, right_rows, ((1,), (1,)))
    squared = left_norms[:, None] + right_norms[None, :] - 2.0 * inner
    return jnp.exp(-jnp.sqrt(squared + softening) / length_scale)


def shards(batch_features, centre_features, targets, weights):
    n_plane, n_ring = lax.axis_size(plane), lax.axis_size(ring)
    own_rows, width = targets.shape
    depth = batch_features.shape[1]
    half = width // 2
    total_rows = own_rows * n_plane * n_ring * 2

    centre = both_cores(gather(centre_features, ring)).reshape(-1, depth)
    batch = both_cores(gather(batch_features, plane)).reshape(-1, depth)
    weight = gather(to_columns(weights), ring)
    weight = weight.transpose(1, 0, 2, 3).reshape(-1, half)
    target = to_columns(targets)
    far = both_cores(lax.all_gather(centre_features, plane, axis=0)).reshape(-1, depth)

    tile = kernel_matrix(batch, centre)
    partial_pred = dot(tile, weight, ((1,), (0,))).reshape(2, n_plane, own_rows, half)
    residual = exchange(partial_pred.transpose(1, 0, 2, 3), plane) - target
    residual_full = gather(residual, plane).transpose(1, 0, 2, 3).reshape(-1, half)
    partial_grad = dot(tile, residual_full, ((0,), (0,))).reshape(2, n_ring, own_rows, half)
    grad = exchange(partial_grad.transpose(1, 0, 2, 3), ring)
    grad_full = gather(grad, ring).transpose(1, 0, 2, 3).reshape(-1, half)

    far_tile = kernel_matrix(far, centre)
    partial_sums = jnp.sum(far_tile, axis=1).reshape(2, n_plane, own_rows)
    row_sums = exchange(partial_sums.transpose(1, 0, 2), plane)
    largest = jnp.max(row_sums).reshape(1, 1)
    largest = jnp.max(gather(largest, plane)).reshape(1, 1)
    largest = jnp.max(gather(largest, ring))

    partial_product = dot(far_tile, grad_full, ((1,), (0,))).reshape(2, n_plane, own_rows, half)
    product = exchange(partial_product.transpose(1, 0, 2, 3), plane)
    step_size = 1.0 / largest
    theta = 2.0 * step_size * grad - step_size * step_size * product
    output_scale = total_rows / math.sqrt(total_rows)
    return to_rows(residual), to_rows(theta * output_scale)


def solution(mesh):
    fine = Mesh(
        mesh.devices.reshape(4, 4, 4, 2, 2),
        ("x", "z_lo", "y", "z_hi", "core"),
    )
    by_batch = P(("x", "z_lo", "y", "z_hi", "core"), None)
    by_centre = P(("y", "z_hi", "core", "x", "z_lo"), None)
    return jax.shard_map(
        shards,
        mesh=fine,
        in_specs=(by_batch, by_centre, by_batch, by_centre),
        out_specs=(by_batch, by_centre),
        check_vma=False,
    )
```

```python
import math

import jax
import jax.numpy as jnp
from jax import lax
from jax.experimental import pallas as pl
from jax.experimental.pallas import tpu as pltpu
from jax.sharding import Mesh
from jax.sharding import PartitionSpec as P

length_scale = 0.5
softening = 0.01
plane = ("x", "y")
ring = ("z_hi", "z_lo")
swap = [(0, 1), (1, 0)]
rider = 8
vmem_bytes = 32 * 1024 * 1024


def whole(space=pltpu.VMEM):
    return pl.BlockSpec(memory_space=space)


def params():
    return pltpu.CompilerParams(vmem_limit_bytes=vmem_bytes)


def cost(flops, moved, transcendentals=0):
    return pl.CostEstimate(flops=flops, bytes_accessed=moved, transcendentals=transcendentals)


def dot(left, right, left_dim, right_dim):
    return lax.dot_general(
        left,
        right,
        (((left_dim,), (right_dim,)), ((), ())),
        precision=lax.Precision.HIGHEST,
        preferred_element_type=jnp.float32,
    )


def right_norms(rows):
    ones = jnp.ones((8, rows.shape[1]), jnp.float32)
    return dot(ones, rows * rows, 1, 1)


def kernel_block(left, right, norms):
    left_norms = jnp.sum(left * left, axis=1, keepdims=True)
    squared = left_norms + norms[:1] - 2.0 * dot(left, right, 1, 1)
    return jnp.exp(-jnp.sqrt(squared + softening) / length_scale)


def flat(value):
    return value.reshape(-1, value.shape[-1])


def predict_kernel(half, left_ref, own_ref, other_ref, mine_ref, *refs):
    tile_ref, pred_ref, norm_ref = refs[-3:]
    rows = own_ref.shape[0]

    @pl.when(pl.program_id(0) == 0)
    def _():
        norm_ref[:, :rows] = right_norms(own_ref[:, half:])
        norm_ref[:, rows:] = right_norms(other_ref[:, half:])

    left = flat(left_ref[...])
    own = kernel_block(left, own_ref[:, half:], norm_ref[:, :rows])
    other = kernel_block(left, other_ref[:, half:], norm_ref[:, rows:])
    tile_ref[:, :rows] = own
    tile_ref[:, rows:] = other
    pred = dot(own, mine_ref[...], 1, 0) + dot(other, other_ref[:, :half], 1, 0)
    pred_ref[...] = pred.reshape(pred_ref.shape)


def predict(left, own, other, mine, place, before=None):
    count, rows, depth = left.shape
    columns, half = 2 * own.shape[0], mine.shape[1]
    step = count // 2
    operands = [left, own, other, mine]
    in_specs = [
        pl.BlockSpec((step, rows, depth), lambda i: (i, 0, 0)),
        pl.BlockSpec(own.shape, lambda i: (0, 0)),
        pl.BlockSpec(other.shape, lambda i: (0, 0)),
        pl.BlockSpec(mine.shape, lambda i: (0, 0)),
    ]
    aliases = {}
    if before is not None:
        operands.append(before)
        in_specs.append(whole(pl.ANY))
        aliases = {4: 1}

    def body(*refs):
        predict_kernel(half, *refs)

    return pl.pallas_call(
        body,
        grid=(2,),
        in_specs=in_specs,
        out_specs=[
            pl.BlockSpec((step * rows, columns), lambda i: (i, 0)),
            pl.BlockSpec((step, 1, rows, half), lambda i: (i, place, 0, 0)),
        ],
        out_shape=[
            jax.ShapeDtypeStruct((count * rows, columns), jnp.float32),
            jax.ShapeDtypeStruct((count, 2, rows, half), jnp.float32),
        ],
        scratch_shapes=[pltpu.VMEM((8, columns), jnp.float32)],
        input_output_aliases=aliases,
        compiler_params=params(),
        cost_estimate=cost(12 * count * rows * columns * (depth + half), 6 * 1024 * 1024, 2 * count * rows * columns),
    )(*operands)


def far_kernel(half, shift_ref, left_ref, own_ref, other_ref, tile_ref, sums_ref, norm_ref, total_ref):
    rows = own_ref.shape[0]

    @pl.when(pl.program_id(0) == 0)
    def _():
        norm_ref[:, :rows] = right_norms(own_ref[:, half:])
        norm_ref[:, rows:] = right_norms(other_ref[:, half:])
        total_ref[...] = jnp.zeros_like(total_ref)

    left = flat(left_ref[...])
    for place, ref in ((0, own_ref), (1, other_ref)):
        columns = pl.ds(place * rows, rows)
        block = kernel_block(left, ref[:, half:], norm_ref[:, columns])
        tile_ref[:, columns] = block
        total_ref[place : place + 1] += jnp.sum(block, axis=0, keepdims=True)
    sums_ref[...] = pltpu.roll(total_ref[...], shift_ref[0], 1)


def far_tile(left, own, other, half, shift):
    count, rows, depth = left.shape
    columns = 2 * own.shape[0]
    step = count // 4

    def body(*refs):
        far_kernel(half, *refs)

    return pl.pallas_call(
        body,
        grid=(4,),
        in_specs=[
            whole(pltpu.SMEM),
            pl.BlockSpec((step, rows, depth), lambda i: (i, 0, 0)),
            pl.BlockSpec(own.shape, lambda i: (0, 0)),
            pl.BlockSpec(other.shape, lambda i: (0, 0)),
        ],
        out_specs=[
            pl.BlockSpec((step * rows, columns), lambda i: (i, 0)),
            pl.BlockSpec((rider, columns // 2), lambda i: (0, 0)),
        ],
        out_shape=[
            jax.ShapeDtypeStruct((count * rows, columns), jnp.float32),
            jax.ShapeDtypeStruct((rider, columns // 2), jnp.float32),
        ],
        scratch_shapes=[pltpu.VMEM((8, columns), jnp.float32), pltpu.VMEM((rider, columns // 2), jnp.float32)],
        compiler_params=params(),
        cost_estimate=cost(12 * count * rows * columns * depth, 7 * 1024 * 1024, 2 * count * rows * columns),
    )(shift, left, own, other)


def settle_kernel(parts_ref, target_ref, residual_ref, copies_ref):
    residual = jnp.sum(parts_ref[...], axis=0) - target_ref[...]
    residual_ref[...] = residual
    copies_ref[...] = jnp.broadcast_to(residual[None], copies_ref.shape)


def settle(parts, target):
    shape = jax.ShapeDtypeStruct
    return pl.pallas_call(
        settle_kernel,
        in_specs=[whole(), whole()],
        out_specs=[whole(), whole()],
        out_shape=[shape(target.shape, jnp.float32), shape(parts.shape, jnp.float32)],
        compiler_params=params(),
        cost_estimate=cost(2 * parts.size, 8 * parts.size),
    )(parts, target)


def gradient_kernel(rows, place_ref, first_ref, second_ref, residual_ref, sums_ref, out_ref):
    count = out_ref.shape[0]
    total = dot(first_ref[...], flat(residual_ref[:, :rows]), 0, 0)
    total += dot(second_ref[...], flat(residual_ref[:, rows:]), 0, 0)
    for step in range(count):
        place = lax.rem(place_ref[0] + step, count)
        out_ref[place, :rows] = total[step * rows : (step + 1) * rows]
        out_ref[place, rows : 2 * rows] = total[(count + step) * rows : (count + step + 1) * rows]
        out_ref[place, 2 * rows :] = sums_ref[...]


def gradient(place, first, second, residual, sums, rows):
    count = first.shape[1] // (2 * rows)
    half = residual.shape[-1]

    def body(*refs):
        gradient_kernel(rows, *refs)

    return pl.pallas_call(
        body,
        in_specs=[whole(pltpu.SMEM)] + [whole()] * 4,
        out_specs=whole(),
        out_shape=jax.ShapeDtypeStruct((count, 2 * rows + rider, half), jnp.float32),
        compiler_params=params(),
        cost_estimate=cost(24 * first.size * half, 4 * 1024 * 1024),
    )(place, first, second, residual, sums)


def collect_kernel(parts_ref, grad_ref, copies_ref, largest_ref):
    rows = grad_ref.shape[0]
    total = jnp.sum(parts_ref[...], axis=0)
    grad_ref[...] = total[:rows]
    copies_ref[...] = jnp.broadcast_to(total[None, :rows], copies_ref.shape)
    largest = jnp.max(jnp.max(total[rows:], axis=0, keepdims=True), axis=1, keepdims=True)
    largest_ref[...] = jnp.broadcast_to(largest, largest_ref.shape)


def collect(parts):
    count, packed, half = parts.shape
    rows = packed - rider
    shape = jax.ShapeDtypeStruct
    return pl.pallas_call(
        collect_kernel,
        in_specs=[whole()],
        out_specs=[whole()] * 3,
        out_shape=[
            shape((rows, half), jnp.float32),
            shape((count, rows, half), jnp.float32),
            shape((rider, half), jnp.float32),
        ],
        compiler_params=params(),
        cost_estimate=cost(2 * parts.size, 8 * parts.size),
    )(parts)


def product_kernel(rows, place_ref, tile_ref, grad_ref, largest_ref, out_ref):
    count = grad_ref.shape[0]
    places = [lax.rem(place_ref[0] + step, count) for step in range(count)]
    own = jnp.concatenate([grad_ref[place, :rows] for place in places], axis=0)
    other = jnp.concatenate([grad_ref[place, rows:] for place in places], axis=0)
    middle, rest = own.shape[0], out_ref.shape[0] * rows
    for core in range(2):
        tile = tile_ref[pl.ds(core * rest, rest), :]
        total = dot(tile[:, :middle], own, 1, 0) + dot(tile[:, middle:], other, 1, 0)
        out_ref[:, core * rows : (core + 1) * rows] = total.reshape(-1, rows, total.shape[-1])
    out_ref[:, 2 * rows :] = jnp.broadcast_to(largest_ref[...][None], (out_ref.shape[0], rider, out_ref.shape[2]))


def product(place, tile, grads, largest, rows):
    half = grads.shape[-1]
    count = tile.shape[0] // (2 * rows)

    def body(*refs):
        product_kernel(rows, *refs)

    return pl.pallas_call(
        body,
        in_specs=[whole(pltpu.SMEM)] + [whole()] * 3,
        out_specs=whole(),
        out_shape=jax.ShapeDtypeStruct((count, 2 * rows + rider, half), jnp.float32),
        compiler_params=params(),
        cost_estimate=cost(12 * tile.size * half, 4 * 1024 * 1024),
    )(place, tile, grads, largest)


def finish_kernel(scale, parts_ref, grad_ref, theta_ref):
    rows = grad_ref.shape[0]
    total = jnp.sum(parts_ref[:, :rows], axis=0)
    largest = jnp.max(parts_ref[:, rows:], axis=0)
    largest = jnp.max(jnp.max(largest, axis=0, keepdims=True), axis=1, keepdims=True)
    step_size = 1.0 / largest
    theta_ref[...] = (2.0 * step_size * grad_ref[...] - step_size * step_size * total) * scale


def finish(parts, grad, scale):
    def body(*refs):
        finish_kernel(scale, *refs)

    return pl.pallas_call(
        body,
        in_specs=[whole(), whole()],
        out_specs=whole(),
        out_shape=jax.ShapeDtypeStruct(grad.shape, jnp.float32),
        compiler_params=params(),
        cost_estimate=cost(2 * parts.size, 4 * parts.size),
    )(parts, grad)


def gather(value, axis):
    copies = jnp.broadcast_to(value[None], (lax.axis_size(axis),) + value.shape)
    return lax.all_to_all(copies, axis, 0, 0)


def ring_pieces(value):
    count, low = lax.axis_size(ring), lax.axis_size("z_lo")

    def slot(place):
        return place % low * (count // low) + place // low

    pieces = [value]
    for step in range(1, count):
        pairs = [(slot(place), slot((place - step) % count)) for place in range(count)]
        pieces.append(lax.ppermute(value, ("z_lo", "z_hi"), pairs))
    return pieces


def from_other(value):
    return lax.ppermute(value, "core", swap)


def halves(rows):
    core = lax.axis_index("core")
    half = rows.shape[1] // 2
    first, second = rows[:, :half], rows[:, half:]
    return jnp.where(core == 0, first, second), jnp.where(core == 0, second, first)


def to_rows(columns):
    core = lax.axis_index("core")
    rows = columns.shape[0] // 2
    own, other = columns[:rows], from_other(columns[rows:])
    first = jnp.where(core == 0, own, other)
    second = jnp.where(core == 0, other, own)
    return jnp.concatenate([first, second], axis=1)


def shards(batch_features, centre_features, targets, weights):
    rows, width = targets.shape
    half = width // 2
    total_rows = rows * lax.axis_size(plane) * lax.axis_size(ring) * 2
    place = lax.axis_index(ring)

    mine, theirs = halves(weights)
    pieces = ring_pieces(jnp.concatenate([theirs, centre_features, mine], axis=1))
    cut = half + centre_features.shape[1]
    batch = gather(batch_features, plane)
    own = jnp.concatenate([piece[:, :cut] for piece in pieces], axis=0)
    mine = jnp.concatenate([piece[:, cut:] for piece in pieces], axis=0)
    other = from_other(own)
    batch_other = from_other(batch)
    later, batch = lax.optimization_barrier((centre_features, batch))
    far = gather(later, plane)
    target_mine, target_theirs = halves(targets)
    target = jnp.concatenate([target_mine, from_other(target_theirs)], axis=0)

    first, pred = predict(batch, own, other, mine, 0)
    second, pred = predict(batch_other, own, other, mine, 1, pred)
    parts = lax.all_to_all(pred.reshape(-1, 2 * rows, half), plane, 0, 0)
    residual, copies = settle(parts, target)
    residual_full = lax.all_to_all(copies, plane, 0, 0)

    far, pred = lax.optimization_barrier((far, pred))
    far = jnp.concatenate([far, from_other(far)], axis=0)
    place_ref = place.reshape(1).astype(jnp.int32)
    tile, sums = far_tile(far, own, other, half, place_ref * rows)

    parts = lax.all_to_all(gradient(place_ref, first, second, residual_full, sums, rows), ring, 0, 0)
    grad, copies, largest = collect(parts)
    grad_full = lax.all_to_all(copies, ring, 0, 0)
    parts = lax.all_to_all(product(place_ref, tile, grad_full, largest, rows), plane, 0, 0)
    theta = finish(parts, grad, total_rows / math.sqrt(total_rows))
    return to_rows(residual), to_rows(theta)


def solution(mesh):
    fine = Mesh(
        mesh.devices.reshape(4, 4, 4, 2, 2),
        ("x", "z_lo", "y", "z_hi", "core"),
    )
    by_batch = P(("x", "z_lo", "y", "z_hi", "core"), None)
    by_centre = P(("y", "z_hi", "core", "x", "z_lo"), None)
    return jax.shard_map(
        shards,
        mesh=fine,
        in_specs=(by_batch, by_centre, by_batch, by_centre),
        out_specs=(by_batch, by_centre),
        check_vma=False,
    )
```

```python
import functools
import math

import jax
import jax.numpy as jnp
from jax import lax
from jax.experimental import pallas as pl
from jax.experimental.pallas import tpu as pltpu
from jax.sharding import Mesh
from jax.sharding import PartitionSpec as P

length_scale = 0.5
softening = 0.01
plane = ("x", "y")
ring = ("z_hi", "z_lo")
swap = [(0, 1), (1, 0)]
rider = 8
vmem_bytes = 24 * 1024 * 1024
most_bytes = 60 * 1024 * 1024


def whole(space=pltpu.VMEM):
    return pl.BlockSpec(memory_space=space)


def params(size=vmem_bytes):
    return pltpu.CompilerParams(vmem_limit_bytes=size)


def shape(sizes, dtype=jnp.float32):
    return jax.ShapeDtypeStruct(sizes, dtype)


def cost(flops, moved, transcendentals=0):
    return pl.CostEstimate(flops=flops, bytes_accessed=moved, transcendentals=transcendentals)


def dot(left, right, left_dim, right_dim):
    return lax.dot_general(
        left,
        right,
        (((left_dim,), (right_dim,)), ((), ())),
        precision=lax.Precision.HIGHEST,
        preferred_element_type=jnp.float32,
    )


def flat(value):
    return value.reshape(-1, value.shape[-1])


def high(value):
    return value.astype(jnp.bfloat16)


def cut(value, count):
    terms = []
    for _ in range(count):
        terms.append(high(value))
        value = value - terms[-1].astype(jnp.float32)
    return terms


def mul(left, right, left_dim, right_dim):
    return lax.dot_general(
        left, right, (((left_dim,), (right_dim,)), ((), ())), preferred_element_type=jnp.float32
    )


def mul_terms(left, right, left_dim, right_dim):
    count = len(left)
    total = None
    for order in reversed(range(count)):
        for place in range(order + 1):
            term = mul(left[place], right[order - place], left_dim, right_dim)
            total = term if total is None else total + term
    return total


def tile_block(left, left_norms, right_refs, norm_ref, columns):
    inner = mul_terms(left, [ref[columns, :] for ref in right_refs], 1, 1)
    squared = left_norms + norm_ref[:1, columns] - 2.0 * inner
    return jnp.exp(-jnp.sqrt(squared + softening) / length_scale)


def square_sums(rows):
    return jnp.sum(rows * rows, axis=1, keepdims=True)


def tile_kernel(half, which, rows_ref, own_ref, other_ref, out_ref, *refs):
    left_ref, right_bufs, right_refs, norm_ref, tile_ref, come, leave = refs[0], refs[1:3], refs[3:6], *refs[6:]
    count, each, depth = left_ref.shape
    moves = []

    def start(source, target):
        moves.append(pltpu.make_async_copy(source, target, come.at[len(moves)]))
        moves[-1].start()

    columns = pl.ds(half, depth)
    start(own_ref.at[:, columns], right_bufs[0])
    middle = count // 2
    for part in (pl.ds(0, middle), pl.ds(middle, count - middle)):
        start(rows_ref.at[part, which], left_ref.at[part])
    start(other_ref.at[:, columns], right_bufs[1])
    gone = []
    for place, move in ((0, moves[0]), (1, moves[3])):
        centres = own_ref.shape[0]
        columns = pl.ds(place * centres, centres)
        move.wait()
        right = right_bufs[place][...]
        for term, ref in zip(cut(right, 3), right_refs):
            ref[columns, :] = term
        ones = jnp.ones((8, depth), jnp.float32)
        norm_ref[:, columns] = dot(ones, right * right, 1, 1)
        if place == 0:
            moves[1].wait()
            moves[2].wait()
            left = flat(left_ref[...])
            left_norms = square_sums(left)
            left = cut(left, 3)
        tile_ref[:, columns] = tile_block(left, left_norms, right_refs, norm_ref, columns)
        gone.append(pltpu.make_async_copy(tile_ref.at[:, columns], out_ref.at[:, columns], leave.at[place]))
        gone[-1].start()
    for move in gone:
        move.wait()


def tile_of(rows, which, own, other, half):
    count, _, each, depth = rows.shape
    columns = 2 * own.shape[0]
    return pl.pallas_call(
        functools.partial(tile_kernel, half, which),
        in_specs=[whole(pl.ANY)] * 3,
        out_specs=whole(pl.ANY),
        out_shape=shape((count * each, columns)),
        scratch_shapes=[pltpu.VMEM((count, each, depth), jnp.float32)]
        + [pltpu.VMEM((columns // 2, depth), jnp.float32)] * 2
        + [pltpu.VMEM((columns, depth), jnp.bfloat16)] * 3
        + [pltpu.VMEM((8, columns), jnp.float32), pltpu.VMEM((count * each, columns), jnp.float32)]
        + [pltpu.SemaphoreType.DMA((4,)), pltpu.SemaphoreType.DMA((2,))],
        compiler_params=params(most_bytes),
        cost_estimate=cost(12 * count * each * columns * depth, 8 * 1024 * 1024, 2 * count * each * columns),
    )(rows, own, other)


def swapped(rows):
    half = rows.shape[-1] // 2
    return jnp.concatenate([rows[:, half:], rows[:, :half]], axis=1)


def predict_kernel(core, tile_ref, mine_ref, held_ref, *refs):
    pred_ref, tile_buf, mine_buf, theirs_buf, pred_buf, come, leave = refs[-7:]
    count, each, half = pred_buf.shape
    pairs = [
        (mine_ref, mine_buf),
        (held_ref.at[:, pl.ds(0, half)], theirs_buf),
        (tile_ref, tile_buf),
    ]
    moves = [pltpu.make_async_copy(*pair, come.at[place]) for place, pair in enumerate(pairs)]
    for move in moves:
        move.start()
    moves[0].wait()
    moves[1].wait()
    weights = [mine_buf[...], theirs_buf[...]]
    if core:
        weights = weights[::-1]
    weights = cut(jnp.concatenate(weights, axis=0), 2)
    moves[2].wait()
    pred_buf[...] = mul_terms(cut(tile_buf[...], 2), weights, 1, 0).reshape(pred_buf.shape)
    move = pltpu.make_async_copy(pred_buf, pred_ref.at[:, pl.ds(core * each, each)], leave)
    move.start()
    move.wait()


def predict(core, tile, mine, held, count, before=()):
    each, half = tile.shape[0] // count, mine.shape[1]
    return pl.pallas_call(
        functools.partial(predict_kernel, core),
        in_specs=[whole(pl.ANY)] * (3 + len(before)),
        out_specs=whole(pl.ANY),
        out_shape=shape((count, 2 * each, half)),
        scratch_shapes=[
            pltpu.VMEM(tile.shape, jnp.float32),
            pltpu.VMEM(mine.shape, jnp.float32),
            pltpu.VMEM(mine.shape, jnp.float32),
            pltpu.VMEM((count, each, half), jnp.float32),
            pltpu.SemaphoreType.DMA((3,)),
            pltpu.SemaphoreType.DMA,
        ],
        input_output_aliases={3: 0} if before else {},
        compiler_params=params(most_bytes),
        cost_estimate=cost(6 * tile.size * half, 3 * 1024 * 1024),
    )(tile, mine, held, *before)


def settle_kernel(parts_ref, target_ref, copies_ref):
    residual = jnp.sum(parts_ref[...], axis=0) - target_ref[...]
    copies_ref[...] = jnp.broadcast_to(residual[None], copies_ref.shape)


def settle(parts, target):
    return pl.pallas_call(
        settle_kernel,
        in_specs=[whole(), whole()],
        out_specs=whole(),
        out_shape=shape(parts.shape),
        compiler_params=params(),
        cost_estimate=cost(2 * parts.size, 8 * parts.size),
    )(parts, target)


def far_terms_kernel(place_ref, own_ref, other_ref, high_ref, low_ref, sums_ref):
    count, columns = own_ref.shape
    total = None
    for core, ref in enumerate((own_ref, other_ref)):
        tile = swapped(ref[...]) if core else ref[...]
        for term, out in zip(cut(tile, 2), (high_ref, low_ref)):
            out[core * count : (core + 1) * count, :] = term
        part = jnp.sum(tile, axis=0, keepdims=True)
        total = part if total is None else total + part
    middle = columns // 2
    sums = [total[:, :middle], total[:, middle:], jnp.zeros((rider - 2, middle), jnp.float32)]
    sums_ref[...] = pltpu.roll(jnp.concatenate(sums, axis=0), place_ref[0], 1)


def far_terms(shift, own, other):
    count, columns = own.shape
    return pl.pallas_call(
        far_terms_kernel,
        in_specs=[whole(pltpu.SMEM), whole(), whole()],
        out_specs=[whole()] * 3,
        out_shape=[shape((2 * count, columns), jnp.bfloat16)] * 2 + [shape((rider, columns // 2))],
        compiler_params=params(),
        cost_estimate=cost(8 * own.size, 16 * own.size),
    )(shift, own, other)


def gradient_kernel(place_ref, own_ref, other_ref, residual_ref, sums_ref, out_ref):
    count = out_ref.shape[0]
    rows = residual_ref.shape[1] // 2
    own = mul_terms(cut(own_ref[...], 2), cut(flat(residual_ref[:, :rows]), 2), 0, 0)
    other = mul_terms(cut(other_ref[...], 2), cut(flat(residual_ref[:, rows:]), 2), 0, 0)
    middle = count * rows
    total = own + jnp.concatenate([other[middle:], other[:middle]], axis=0)
    for step in range(count):
        place = lax.rem(place_ref[0] + step, count)
        out_ref[place, :rows] = total[step * rows : (step + 1) * rows]
        out_ref[place, rows : 2 * rows] = total[middle + step * rows : middle + (step + 1) * rows]
        out_ref[place, 2 * rows :] = sums_ref[...]


def gradient(place, tiles, residual, sums):
    _, rows, half = residual.shape
    count = tiles[0].shape[1] // rows
    return pl.pallas_call(
        gradient_kernel,
        in_specs=[whole(pltpu.SMEM)] + [whole()] * 4,
        out_specs=whole(),
        out_shape=shape((count, rows + rider, half)),
        compiler_params=params(),
        cost_estimate=cost(12 * tiles[0].size * half, 4 * 1024 * 1024),
    )(place, *tiles, residual, sums)


def collect_kernel(parts_ref, grad_ref, copies_ref, largest_ref):
    rows = grad_ref.shape[0]
    total = jnp.sum(parts_ref[...], axis=0)
    grad_ref[...] = total[:rows]
    copies_ref[...] = jnp.broadcast_to(total[None, :rows], copies_ref.shape)
    largest = jnp.max(jnp.max(total[rows:], axis=0, keepdims=True), axis=1, keepdims=True)
    largest_ref[...] = jnp.broadcast_to(largest, largest_ref.shape)


def collect(parts):
    count, packed, half = parts.shape
    rows = packed - rider
    return pl.pallas_call(
        collect_kernel,
        in_specs=[whole()],
        out_specs=[whole()] * 3,
        out_shape=[
            shape((rows, half), jnp.float32),
            shape((count, rows, half), jnp.float32),
            shape((rider, half), jnp.float32),
        ],
        compiler_params=params(),
        cost_estimate=cost(2 * parts.size, 8 * parts.size),
    )(parts)


def product_kernel(place_ref, high_ref, low_ref, grad_ref, largest_ref, out_ref):
    count, rows, half = grad_ref.shape
    rows = rows // 2
    places = [lax.rem(place_ref[0] + step, count) for step in range(count)]
    grads = [grad_ref[place, :rows] for place in places] + [grad_ref[place, rows:] for place in places]
    total = mul_terms([high_ref[...], low_ref[...]], cut(jnp.concatenate(grads, axis=0), 2), 1, 0)
    middle = total.shape[0] // 2
    for core in range(2):
        part = total[core * middle : (core + 1) * middle]
        out_ref[:, core * rows : (core + 1) * rows] = part.reshape(-1, rows, half)
    out_ref[:, 2 * rows :] = jnp.broadcast_to(largest_ref[...][None], (out_ref.shape[0], rider, half))


def product(place, terms, grads, largest):
    _, rows, half = grads.shape
    count = terms[0].shape[0] // rows
    return pl.pallas_call(
        product_kernel,
        in_specs=[whole(pltpu.SMEM)] + [whole()] * 4,
        out_specs=whole(),
        out_shape=shape((count, rows + rider, half)),
        compiler_params=params(),
        cost_estimate=cost(6 * terms[0].size * half, 4 * 1024 * 1024),
    )(place, *terms, grads, largest)


def finish_kernel(scale, parts_ref, grad_ref, theta_ref):
    rows = grad_ref.shape[0]
    total = jnp.sum(parts_ref[:, :rows], axis=0)
    largest = jnp.max(parts_ref[:, rows:], axis=0)
    largest = jnp.max(jnp.max(largest, axis=0, keepdims=True), axis=1, keepdims=True)
    step_size = 1.0 / largest
    theta_ref[...] = (2.0 * step_size * grad_ref[...] - step_size * step_size * total) * scale


def finish(parts, grad, scale):
    def body(*refs):
        finish_kernel(scale, *refs)

    return pl.pallas_call(
        body,
        in_specs=[whole(), whole()],
        out_specs=whole(),
        out_shape=shape(grad.shape),
        compiler_params=params(),
        cost_estimate=cost(2 * parts.size, 4 * parts.size),
    )(parts, grad)


def assemble_kernel(count, *refs):
    own_ref, mine_ref = refs[count:]
    for place, ref in enumerate(refs[:count]):
        rows = ref.shape[0]
        edge = own_ref.shape[1]
        own_ref[place * rows : (place + 1) * rows, :] = ref[:, :edge]
        mine_ref[place * rows : (place + 1) * rows, :] = ref[:, edge:]


def assemble(pieces, edge):
    count = len(pieces)
    rows, width = pieces[0].shape

    def body(*refs):
        assemble_kernel(count, *refs)

    return pl.pallas_call(
        body,
        in_specs=[whole()] * count,
        out_specs=[whole()] * 2,
        out_shape=[
            shape((count * rows, edge)),
            shape((count * rows, width - edge)),
        ],
        compiler_params=params(),
        cost_estimate=cost(0, 8 * count * rows * width),
    )(*pieces)


def gather(value, axis):
    copies = jnp.broadcast_to(value[None], (lax.axis_size(axis),) + value.shape)
    return lax.all_to_all(copies, axis, 0, 0)


def ring_pieces(value):
    count, low = lax.axis_size(ring), lax.axis_size("z_lo")

    def slot(place):
        return place % low * (count // low) + place // low

    def hop(held, step):
        pairs = [(slot(place), slot((place + step) % count)) for place in range(count)]
        return lax.ppermute(held, ("z_lo", "z_hi"), pairs)

    ahead, behind = [value], [value]
    for step in range(1, count):
        if step % 2:
            behind.append(hop(behind[-1], 1))
        else:
            ahead.append(hop(ahead[-1], -1))
    return ahead + behind[:0:-1]


def from_other(value):
    return lax.ppermute(value, "core", swap)


def halves(rows):
    core = lax.axis_index("core")
    half = rows.shape[1] // 2
    first, second = rows[:, :half], rows[:, half:]
    return jnp.where(core == 0, first, second), jnp.where(core == 0, second, first)


def to_rows(*columns):
    core = lax.axis_index("core")
    rows = columns[0].shape[0] // 2
    own = jnp.concatenate([value[:rows] for value in columns], axis=0)
    other = from_other(jnp.concatenate([value[rows:] for value in columns], axis=0))
    first = jnp.where(core == 0, own, other)
    second = jnp.where(core == 0, other, own)
    both = jnp.concatenate([first, second], axis=1)
    return tuple(both[place * rows : (place + 1) * rows] for place in range(len(columns)))


def shards(batch_features, centre_features, targets, weights):
    rows, width = targets.shape
    half = width // 2
    total_rows = rows * lax.axis_size(plane) * lax.axis_size(ring) * 2
    place = lax.axis_index(ring)

    count = lax.axis_size(plane)
    place = place.reshape(1).astype(jnp.int32)

    mine, theirs = halves(weights)
    pieces = ring_pieces(jnp.concatenate([theirs, centre_features, mine], axis=1))
    features = jnp.stack([batch_features, centre_features])
    features = jnp.broadcast_to(features[None], (count,) + features.shape)
    features = lax.all_to_all(features, plane, 0, 0)
    target_mine, target_theirs = halves(targets)
    target = jnp.concatenate([target_mine, from_other(target_theirs)], axis=0)
    own, mine = assemble(pieces, half + centre_features.shape[1])
    other = from_other(own)

    tile = tile_of(features, 0, own, other, half)
    tiles = tile, from_other(tile)
    pred = predict(0, tiles[0], mine, other, count)
    pred = predict(1, tiles[1], mine, other, count, (pred,))
    far = tile_of(features, 1, own, other, half)
    *fars, sums = far_terms(place * rows, far, from_other(far))
    parts = lax.all_to_all(pred, plane, 0, 0)
    residuals = settle(parts, target)
    residual_full = lax.all_to_all(residuals, plane, 0, 0)
    parts = lax.all_to_all(gradient(place, tiles, residual_full, sums), ring, 0, 0)
    grad, copies, largest = collect(parts)
    grad_full = lax.all_to_all(copies, ring, 0, 0)
    parts = lax.all_to_all(product(place, fars, grad_full, largest), plane, 0, 0)
    theta = finish(parts, grad, total_rows / math.sqrt(total_rows))
    return to_rows(residuals[0], theta)


def solution(mesh):
    fine = Mesh(
        mesh.devices.reshape(4, 4, 4, 2, 2),
        ("x", "z_lo", "y", "z_hi", "core"),
    )
    by_batch = P(("x", "z_lo", "y", "z_hi", "core"), None)
    by_centre = P(("y", "z_hi", "core", "x", "z_lo"), None)
    return jax.shard_map(
        shards,
        mesh=fine,
        in_specs=(by_batch, by_centre, by_batch, by_centre),
        out_specs=(by_batch, by_centre),
        check_vma=False,
    )
```

```python
import functools
import math

import jax
import jax.numpy as jnp
from jax import lax
from jax.experimental import pallas as pl
from jax.experimental.pallas import tpu as pltpu
from jax.sharding import Mesh
from jax.sharding import PartitionSpec as P

length_scale = 0.5
softening = 0.01
plane = ("x", "y")
ring = ("z_hi", "z_lo")
swap = [(0, 1), (1, 0)]
rider = 8
vmem_bytes = 24 * 1024 * 1024
most_bytes = 60 * 1024 * 1024


def whole(space=pltpu.VMEM):
    return pl.BlockSpec(memory_space=space)


def params(size=vmem_bytes):
    return pltpu.CompilerParams(vmem_limit_bytes=size)


def shape(sizes, dtype=jnp.float32):
    return jax.ShapeDtypeStruct(sizes, dtype)


def cost(flops, moved, transcendentals=0):
    return pl.CostEstimate(flops=flops, bytes_accessed=moved, transcendentals=transcendentals)


def dot(left, right, left_dim, right_dim):
    return lax.dot_general(
        left,
        right,
        (((left_dim,), (right_dim,)), ((), ())),
        precision=lax.Precision.HIGHEST,
        preferred_element_type=jnp.float32,
    )


def flat(value):
    return value.reshape(-1, value.shape[-1])


def high(value):
    return value.astype(jnp.bfloat16)


def cut(value, count):
    terms = []
    for _ in range(count):
        terms.append(high(value))
        value = value - terms[-1].astype(jnp.float32)
    return terms


def mul(left, right, left_dim, right_dim):
    return lax.dot_general(
        left, right, (((left_dim,), (right_dim,)), ((), ())), preferred_element_type=jnp.float32
    )


def mul_terms(left, right, left_dim, right_dim):
    count = len(left)
    total = None
    for order in reversed(range(count)):
        for place in range(order + 1):
            term = mul(left[place], right[order - place], left_dim, right_dim)
            total = term if total is None else total + term
    return total


def tile_block(left, left_norms, right_refs, norm_ref, columns):
    inner = mul_terms(left, [ref[columns, :] for ref in right_refs], 1, 1)
    squared = left_norms + norm_ref[:1, columns] - 2.0 * inner
    return jnp.exp(-jnp.sqrt(squared + softening) / length_scale)


def square_sums(rows):
    return jnp.sum(rows * rows, axis=1, keepdims=True)


def tile_kernel(half, shared, own_ref, other_ref, packed_ref, *refs):
    outs, refs = refs[: 1 + shared], refs[1 + shared :]
    left_ref, right_refs, rights, norm_ref, tile_ref, come, leave = refs[0], refs[1:3], refs[3:6], *refs[6:10]
    count, each, width = packed_ref.shape
    rows, depth = own_ref.shape
    step = count // 2
    centre_ref = packed_ref.at[:, :, pl.ds(half, depth)]
    pairs = [
        (centre_ref.at[pl.ds(0, step)], right_refs[0]),
        (own_ref, left_ref.at[pl.ds(0, rows)]),
        (other_ref, left_ref.at[pl.ds(rows, rows)]),
        (centre_ref.at[pl.ds(step, step)], right_refs[1]),
    ]
    if shared:
        weight_refs, share_refs = refs[10:12], refs[12:14]
        for place, columns in enumerate((pl.ds(0, half), pl.ds(width - half, half))):
            pairs.append((packed_ref.at[:, :, columns], weight_refs[place]))
    moves = [pltpu.make_async_copy(*pair, come.at[place]) for place, pair in enumerate(pairs)]
    for move in moves:
        move.start()
    shares, gone = [None] * shared, []

    def send(source, target):
        gone.append(pltpu.make_async_copy(source, target, leave.at[len(gone)]))
        gone[-1].start()

    for place, move in ((0, moves[0]), (1, moves[3])):
        columns = pl.ds(place * step * each, step * each)
        move.wait()
        right = flat(right_refs[place][...])
        for term, ref in zip(cut(right, 3), rights):
            ref[columns, :] = term
        ones = jnp.ones((8, depth), jnp.float32)
        norm_ref[:, columns] = dot(ones, right * right, 1, 1)
        if place == 0:
            moves[1].wait()
            moves[2].wait()
            left = left_ref[...]
            left_norms = square_sums(left)
            left = cut(left, 3)
        block = tile_block(left, left_norms, rights, norm_ref, columns)
        tile_ref[:, columns] = block
        send(tile_ref.at[:, columns], outs[0].at[:, columns])
        if shared:
            if place == 0:
                moves[4].wait()
                moves[5].wait()
            terms = cut(block, 2)
            for part, ref in enumerate(weight_refs):
                weights = cut(flat(ref[place * step : (place + 1) * step]), 2)
                share = mul_terms(terms, weights, 1, 0)
                shares[part] = share if shares[part] is None else shares[part] + share
    for part in range(shared):
        share_refs[part][...] = shares[part]
        send(share_refs[part], outs[1 + part])
    for move in gone:
        move.wait()


def tile_of(own, other, packed, half, shared=0):
    count, each, _ = packed.shape
    rows, depth = own.shape
    rows, columns = 2 * rows, count * each
    scratch = [pltpu.VMEM((rows, depth), jnp.float32)]
    scratch += [pltpu.VMEM((count // 2, each, depth), jnp.float32)] * 2
    scratch += [pltpu.VMEM((columns, depth), jnp.bfloat16)] * 3
    scratch += [pltpu.VMEM((8, columns), jnp.float32), pltpu.VMEM((rows, columns), jnp.float32)]
    scratch += [pltpu.SemaphoreType.DMA((4 + shared,)), pltpu.SemaphoreType.DMA((2 + shared,))]
    scratch += [pltpu.VMEM((count, each, half), jnp.float32)] * shared
    scratch += [pltpu.VMEM((rows, half), jnp.float32)] * shared
    return pl.pallas_call(
        functools.partial(tile_kernel, half, shared),
        in_specs=[whole(pl.ANY)] * 3,
        out_specs=[whole(pl.ANY)] * (1 + shared),
        out_shape=[shape((rows, columns))] + [shape((rows, half))] * shared,
        scratch_shapes=scratch,
        compiler_params=params(most_bytes),
        cost_estimate=cost(12 * rows * columns * depth, 6 * 1024 * 1024, 2 * rows * columns),
    )(own, other, packed)


def swapped(rows):
    half = rows.shape[0] // 2
    return jnp.concatenate([rows[half:], rows[:half]], axis=0)


def ring_places(place_ref, count):
    return [lax.rem(place_ref[0] + step, count) for step in range(count)]


def from_ring(ref, places, rows):
    mine = [ref[place, :rows] for place in places]
    return jnp.concatenate(mine + [ref[place, rows : 2 * rows] for place in places], axis=0)


def to_ring(total, ref, places, rows):
    middle = total.shape[0] // 2
    for step, place in enumerate(places):
        ref[place, :rows] = total[step * rows : (step + 1) * rows]
        ref[place, rows : 2 * rows] = total[middle + step * rows : middle + (step + 1) * rows]


def join_kernel(place_ref, own_ref, other_ref, pred_ref):
    count, rows, _ = pred_ref.shape
    to_ring(own_ref[...] + swapped(other_ref[...]), pred_ref, ring_places(place_ref, count), rows // 2)


def join(place, own, other, rows):
    count, half = own.shape
    return pl.pallas_call(
        join_kernel,
        in_specs=[whole(pltpu.SMEM), whole(), whole()],
        out_specs=whole(),
        out_shape=shape((count // (2 * rows), 2 * rows, half)),
        compiler_params=params(),
        cost_estimate=cost(own.size, 12 * own.size),
    )(place, own, other)


def settle_kernel(parts_ref, target_ref, copies_ref):
    residual = jnp.sum(parts_ref[...], axis=0) - target_ref[...]
    copies_ref[...] = jnp.broadcast_to(residual[None], copies_ref.shape)


def settle(parts, target):
    return pl.pallas_call(
        settle_kernel,
        in_specs=[whole(), whole()],
        out_specs=whole(),
        out_shape=shape(parts.shape),
        compiler_params=params(),
        cost_estimate=cost(2 * parts.size, 8 * parts.size),
    )(parts, target)


def far_terms_kernel(own_ref, other_ref, high_ref, low_ref, sums_ref):
    columns, width = own_ref.shape[1], sums_ref.shape[1]
    lines = []
    for core, ref in enumerate((own_ref, other_ref)):
        tile = swapped(ref[...]) if core else ref[...]
        for term, out in zip(cut(tile, 2), (high_ref, low_ref)):
            out[:, core * columns : (core + 1) * columns] = term
        part = jnp.sum(tile, axis=0, keepdims=True)
        lines += [part[:, place : place + width] for place in range(0, columns, width)]
    lines.append(jnp.zeros((rider - len(lines), width), jnp.float32))
    sums_ref[...] = jnp.concatenate(lines, axis=0)


def far_terms(own, other, half):
    rows, columns = own.shape
    return pl.pallas_call(
        far_terms_kernel,
        in_specs=[whole(), whole()],
        out_specs=[whole()] * 3,
        out_shape=[shape((rows, 2 * columns), jnp.bfloat16)] * 2 + [shape((rider, half))],
        compiler_params=params(),
        cost_estimate=cost(8 * own.size, 16 * own.size),
    )(own, other)


def gradient_kernel(place_ref, own_ref, other_ref, residual_ref, sums_ref, out_ref):
    count, rows, half = residual_ref.shape
    rows = rows // 2
    residual = from_ring(residual_ref, ring_places(place_ref, count), rows)
    own = mul_terms(cut(own_ref[...], 2), cut(residual, 2), 0, 0)
    other = mul_terms(cut(other_ref[...], 2), cut(swapped(residual), 2), 0, 0)
    out_ref[:, :rows] = own.reshape(-1, rows, half)
    out_ref[:, rows : 2 * rows] = other.reshape(-1, rows, half)
    out_ref[:, 2 * rows :] = jnp.broadcast_to(sums_ref[...][None], (out_ref.shape[0], rider, half))


def gradient(place, tiles, residual, sums):
    _, rows, half = residual.shape
    count = 2 * tiles[0].shape[1] // rows
    return pl.pallas_call(
        gradient_kernel,
        in_specs=[whole(pltpu.SMEM)] + [whole()] * 4,
        out_specs=whole(),
        out_shape=shape((count, rows + rider, half)),
        compiler_params=params(),
        cost_estimate=cost(12 * tiles[0].size * half, 4 * 1024 * 1024),
    )(place, *tiles, residual, sums)


def collect_kernel(parts_ref, grad_ref, copies_ref, largest_ref):
    rows = grad_ref.shape[0]
    total = jnp.sum(parts_ref[...], axis=0)
    grad_ref[...] = total[:rows]
    copies_ref[...] = jnp.broadcast_to(total[None, :rows], copies_ref.shape)
    largest = jnp.max(jnp.max(total[rows:], axis=0, keepdims=True), axis=1, keepdims=True)
    largest_ref[...] = jnp.broadcast_to(largest, largest_ref.shape)


def collect(parts):
    count, packed, half = parts.shape
    rows = packed - rider
    return pl.pallas_call(
        collect_kernel,
        in_specs=[whole()],
        out_specs=[whole()] * 3,
        out_shape=[
            shape((rows, half), jnp.float32),
            shape((count, rows, half), jnp.float32),
            shape((rider, half), jnp.float32),
        ],
        compiler_params=params(),
        cost_estimate=cost(2 * parts.size, 8 * parts.size),
    )(parts)


def product_kernel(place_ref, high_ref, low_ref, grad_ref, largest_ref, out_ref):
    rows = grad_ref.shape[1] // 2
    count, _, half = out_ref.shape
    grads = jnp.concatenate([flat(grad_ref[:, :rows]), flat(grad_ref[:, rows:])], axis=0)
    total = mul_terms([high_ref[...], low_ref[...]], cut(grads, 2), 1, 0)
    to_ring(total, out_ref, ring_places(place_ref, count), rows)
    out_ref[:, 2 * rows :] = jnp.broadcast_to(largest_ref[...][None], (count, rider, half))


def product(place, terms, grads, largest):
    _, rows, half = grads.shape
    count = terms[0].shape[0] // rows
    return pl.pallas_call(
        product_kernel,
        in_specs=[whole(pltpu.SMEM)] + [whole()] * 4,
        out_specs=whole(),
        out_shape=shape((count, rows + rider, half)),
        compiler_params=params(),
        cost_estimate=cost(6 * terms[0].size * half, 4 * 1024 * 1024),
    )(place, *terms, grads, largest)


def finish_kernel(scale, parts_ref, grad_ref, theta_ref):
    rows = grad_ref.shape[0]
    total = jnp.sum(parts_ref[:, :rows], axis=0)
    largest = jnp.max(parts_ref[:, rows:], axis=0)
    largest = jnp.max(jnp.max(largest, axis=0, keepdims=True), axis=1, keepdims=True)
    step_size = 1.0 / largest
    theta_ref[...] = (2.0 * step_size * grad_ref[...] - step_size * step_size * total) * scale


def finish(parts, grad, scale):
    def body(*refs):
        finish_kernel(scale, *refs)

    return pl.pallas_call(
        body,
        in_specs=[whole(), whole()],
        out_specs=whole(),
        out_shape=shape(grad.shape),
        compiler_params=params(),
        cost_estimate=cost(2 * parts.size, 4 * parts.size),
    )(parts, grad)


def spread_kernel(core_ref, weight_ref, centre_ref, out_ref, packed_ref, semaphores):
    half, width = weight_ref.shape[1] // 2, packed_ref.shape[1]
    packed_ref[:, half : width - half] = centre_ref[...]
    first, second = weight_ref[:, :half], weight_ref[:, half:]
    low = core_ref[0] == 0
    packed_ref[:, :half] = jnp.where(low, second, first)
    packed_ref[:, width - half :] = jnp.where(low, first, second)
    moves = [
        pltpu.make_async_copy(packed_ref, out_ref.at[place], semaphores.at[place]) for place in range(out_ref.shape[0])
    ]
    for move in moves:
        move.start()
    for move in moves:
        move.wait()


def spread(weights, centres, count):
    rows, width = weights.shape[0], weights.shape[1] + centres.shape[1]
    return pl.pallas_call(
        spread_kernel,
        in_specs=[whole(pltpu.SMEM), whole(), whole()],
        out_specs=whole(pl.ANY),
        out_shape=shape((count, rows, width)),
        scratch_shapes=[pltpu.VMEM((rows, width), jnp.float32), pltpu.SemaphoreType.DMA((count,))],
        compiler_params=params(most_bytes),
        cost_estimate=cost(0, 4 * count * rows * width),
    )(lax.axis_index("core").reshape(1).astype(jnp.int32), weights, centres)


def assemble_kernel(count, *refs):
    for place, ref in enumerate(refs[:count]):
        rows = ref.shape[0] // 2
        for part, out_ref in enumerate(refs[count:]):
            out_ref[place * rows : (place + 1) * rows, :] = ref[part * rows : (part + 1) * rows, :]


def assemble(pieces):
    count = len(pieces)
    rows, width = pieces[0].shape
    return pl.pallas_call(
        functools.partial(assemble_kernel, count),
        in_specs=[whole()] * count,
        out_specs=[whole()] * 2,
        out_shape=[shape((count * rows // 2, width))] * 2,
        compiler_params=params(),
        cost_estimate=cost(0, 8 * count * rows * width),
    )(*pieces)


def gather(value, axis):
    copies = jnp.broadcast_to(value[None], (lax.axis_size(axis),) + value.shape)
    return lax.all_to_all(copies, axis, 0, 0)


def ring_pieces(value):
    count, low = lax.axis_size(ring), lax.axis_size("z_lo")

    def slot(place):
        return place % low * (count // low) + place // low

    def hop(held, step):
        pairs = [(slot(place), slot((place + step) % count)) for place in range(count)]
        return lax.ppermute(held, ("z_lo", "z_hi"), pairs)

    ahead, behind = [value], [value]
    for step in range(1, count):
        if step % 2:
            behind.append(hop(behind[-1], 1))
        else:
            ahead.append(hop(ahead[-1], -1))
    return ahead + behind[:0:-1]


def from_other(value):
    return lax.ppermute(value, "core", swap)


def halves(rows):
    core = lax.axis_index("core")
    half = rows.shape[1] // 2
    first, second = rows[:, :half], rows[:, half:]
    return jnp.where(core == 0, first, second), jnp.where(core == 0, second, first)


def to_rows(*columns):
    core = lax.axis_index("core")
    rows = columns[0].shape[0] // 2
    own = jnp.concatenate([value[:rows] for value in columns], axis=0)
    other = from_other(jnp.concatenate([value[rows:] for value in columns], axis=0))
    first = jnp.where(core == 0, own, other)
    second = jnp.where(core == 0, other, own)
    both = jnp.concatenate([first, second], axis=1)
    return tuple(both[place * rows : (place + 1) * rows] for place in range(len(columns)))


def shards(batch_features, centre_features, targets, weights):
    rows, width = targets.shape
    half = width // 2
    total_rows = rows * lax.axis_size(plane) * lax.axis_size(ring) * 2
    place = lax.axis_index(ring)

    place = place.reshape(1).astype(jnp.int32)

    centres = spread(weights, centre_features, lax.axis_size(plane))
    centres = lax.all_to_all(centres, plane, 0, 0)
    pieces = ring_pieces(jnp.concatenate([batch_features, centre_features], axis=0))
    batch, far = assemble(pieces)
    batch_other = from_other(batch)
    far_other = from_other(far)
    tile, theirs, mine = tile_of(batch, batch_other, centres, half, 2)
    pred = join(place, mine, from_other(theirs), rows)
    tiles = tile, from_other(tile)
    target_mine, target_theirs = halves(targets)
    target = jnp.concatenate([target_mine, from_other(target_theirs)], axis=0)
    parts = lax.all_to_all(pred, ring, 0, 0)
    residuals = settle(parts, target)
    residual_full = lax.all_to_all(residuals, ring, 0, 0)

    (far_tile,) = tile_of(far, far_other, centres, half)
    *fars, sums = far_terms(far_tile, from_other(far_tile), half)
    parts = lax.all_to_all(gradient(place, tiles, residual_full, sums), plane, 0, 0)
    grad, copies, largest = collect(parts)
    grad_full = lax.all_to_all(copies, plane, 0, 0)
    parts = lax.all_to_all(product(place, fars, grad_full, largest), ring, 0, 0)
    theta = finish(parts, grad, total_rows / math.sqrt(total_rows))
    return to_rows(residuals[0], theta)


def solution(mesh):
    fine = Mesh(
        mesh.devices.reshape(4, 4, 4, 2, 2),
        ("x", "z_lo", "y", "z_hi", "core"),
    )
    by_batch = P(("x", "z_lo", "y", "z_hi", "core"), None)
    by_centre = P(("y", "z_hi", "core", "x", "z_lo"), None)
    return jax.shard_map(
        shards,
        mesh=fine,
        in_specs=(by_batch, by_centre, by_batch, by_centre),
        out_specs=(by_batch, by_centre),
        check_vma=False,
    )
```

```python
import functools
import math

import jax
import jax.numpy as jnp
from jax import lax
from jax.experimental import pallas as pl
from jax.experimental.pallas import tpu as pltpu
from jax.sharding import Mesh
from jax.sharding import PartitionSpec as P

length_scale = 0.5
softening = 0.01
plane = ("x", "y")
ring = ("z_hi", "z_lo")
swap = [(0, 1), (1, 0)]
rider = 8
vmem_bytes = 24 * 1024 * 1024
most_bytes = 60 * 1024 * 1024


def whole(space=pltpu.VMEM):
    return pl.BlockSpec(memory_space=space)


def params(size=vmem_bytes):
    return pltpu.CompilerParams(vmem_limit_bytes=size)


def shape(sizes, dtype=jnp.float32):
    return jax.ShapeDtypeStruct(sizes, dtype)


def cost(flops, moved, transcendentals=0):
    return pl.CostEstimate(flops=flops, bytes_accessed=moved, transcendentals=transcendentals)


def dot(left, right, left_dim, right_dim):
    return lax.dot_general(
        left,
        right,
        (((left_dim,), (right_dim,)), ((), ())),
        precision=lax.Precision.HIGHEST,
        preferred_element_type=jnp.float32,
    )


def flat(value):
    return value.reshape(-1, value.shape[-1])


def high(value):
    return value.astype(jnp.bfloat16)


def cut(value, count):
    terms = []
    for _ in range(count):
        terms.append(high(value))
        value = value - terms[-1].astype(jnp.float32)
    return terms


def mul(left, right, left_dim, right_dim):
    return lax.dot_general(
        left, right, (((left_dim,), (right_dim,)), ((), ())), preferred_element_type=jnp.float32
    )


def mul_terms(left, right, left_dim, right_dim):
    count = len(left)
    total = None
    for order in reversed(range(count)):
        for place in range(order + 1):
            term = mul(left[place], right[order - place], left_dim, right_dim)
            total = term if total is None else total + term
    return total


def tile_block(left, left_norms, right_refs, norm_ref, columns):
    inner = mul_terms(left, [ref[columns, :] for ref in right_refs], 1, 1)
    squared = left_norms + norm_ref[:1, columns] - 2.0 * inner
    return jnp.exp(-jnp.sqrt(squared + softening) / length_scale)


def square_sums(rows):
    return jnp.sum(rows * rows, axis=1, keepdims=True)


def tile_kernel(half, shared, own_ref, other_ref, packed_ref, *refs):
    outs, refs = refs[: 1 + shared], refs[1 + shared :]
    left_ref, right_refs, rights, norm_ref, tile_ref, come, leave = refs[0], refs[1:3], refs[3:6], *refs[6:10]
    count, each, width = packed_ref.shape
    rows, depth = own_ref.shape
    step = count // 2
    centre_ref = packed_ref.at[:, :, pl.ds(half, depth)]
    pairs = [
        (centre_ref.at[pl.ds(0, step)], right_refs[0]),
        (own_ref, left_ref.at[pl.ds(0, rows)]),
        (other_ref, left_ref.at[pl.ds(rows, rows)]),
        (centre_ref.at[pl.ds(step, step)], right_refs[1]),
    ]
    if shared:
        weight_refs, share_refs = refs[10:12], refs[12:14]
        for place, columns in enumerate((pl.ds(0, half), pl.ds(width - half, half))):
            pairs.append((packed_ref.at[:, :, columns], weight_refs[place]))
    moves = [pltpu.make_async_copy(*pair, come.at[place]) for place, pair in enumerate(pairs)]
    for move in moves:
        move.start()
    shares, gone = [None] * shared, []

    def send(source, target):
        gone.append(pltpu.make_async_copy(source, target, leave.at[len(gone)]))
        gone[-1].start()

    for place, move in ((0, moves[0]), (1, moves[3])):
        columns = pl.ds(place * step * each, step * each)
        move.wait()
        right = flat(right_refs[place][...])
        for term, ref in zip(cut(right, 3), rights):
            ref[columns, :] = term
        ones = jnp.ones((8, depth), jnp.float32)
        norm_ref[:, columns] = dot(ones, right * right, 1, 1)
        if place == 0:
            moves[1].wait()
            moves[2].wait()
            left = left_ref[...]
            left_norms = square_sums(left)
            left = cut(left, 3)
        block = tile_block(left, left_norms, rights, norm_ref, columns)
        tile_ref[:, columns] = block
        send(tile_ref.at[:, columns], outs[0].at[:, columns])
        if shared:
            if place == 0:
                moves[4].wait()
                moves[5].wait()
            terms = cut(block, 2)
            for part, ref in enumerate(weight_refs):
                weights = cut(flat(ref[place * step : (place + 1) * step]), 2)
                share = mul_terms(terms, weights, 1, 0)
                shares[part] = share if shares[part] is None else shares[part] + share
    for part in range(shared):
        share_refs[part][...] = shares[part]
        send(share_refs[part], outs[1 + part])
    for move in gone:
        move.wait()


def tile_of(own, other, packed, half, shared=0):
    count, each, _ = packed.shape
    rows, depth = own.shape
    rows, columns = 2 * rows, count * each
    scratch = [pltpu.VMEM((rows, depth), jnp.float32)]
    scratch += [pltpu.VMEM((count // 2, each, depth), jnp.float32)] * 2
    scratch += [pltpu.VMEM((columns, depth), jnp.bfloat16)] * 3
    scratch += [pltpu.VMEM((8, columns), jnp.float32), pltpu.VMEM((rows, columns), jnp.float32)]
    scratch += [pltpu.SemaphoreType.DMA((4 + shared,)), pltpu.SemaphoreType.DMA((2 + shared,))]
    scratch += [pltpu.VMEM((count, each, half), jnp.float32)] * shared
    scratch += [pltpu.VMEM((rows, half), jnp.float32)] * shared
    return pl.pallas_call(
        functools.partial(tile_kernel, half, shared),
        in_specs=[whole(pl.ANY)] * 3,
        out_specs=[whole(pl.ANY)] * (1 + shared),
        out_shape=[shape((rows, columns))] + [shape((rows, half))] * shared,
        scratch_shapes=scratch,
        compiler_params=params(most_bytes),
        cost_estimate=cost(12 * rows * columns * depth, 6 * 1024 * 1024, 2 * rows * columns),
    )(own, other, packed)


def swapped(rows):
    half = rows.shape[0] // 2
    return jnp.concatenate([rows[half:], rows[:half]], axis=0)


def ring_places(place_ref, count):
    return [lax.rem(place_ref[0] + step, count) for step in range(count)]


def from_ring(ref, places, rows):
    mine = [ref[place, :rows] for place in places]
    return jnp.concatenate(mine + [ref[place, rows : 2 * rows] for place in places], axis=0)


def to_ring(total, ref, places, rows):
    middle = total.shape[0] // 2
    for step, place in enumerate(places):
        ref[place, :rows] = total[step * rows : (step + 1) * rows]
        ref[place, rows : 2 * rows] = total[middle + step * rows : middle + (step + 1) * rows]


def join_kernel(place_ref, own_ref, other_ref, pred_ref):
    count, rows, _ = pred_ref.shape
    to_ring(own_ref[...] + swapped(other_ref[...]), pred_ref, ring_places(place_ref, count), rows // 2)


def join(place, own, other, rows):
    count, half = own.shape
    return pl.pallas_call(
        join_kernel,
        in_specs=[whole(pltpu.SMEM), whole(), whole()],
        out_specs=whole(),
        out_shape=shape((count // (2 * rows), 2 * rows, half)),
        compiler_params=params(),
        cost_estimate=cost(own.size, 12 * own.size),
    )(place, own, other)


def settle_kernel(parts_ref, target_ref, copies_ref):
    residual = jnp.sum(parts_ref[...], axis=0) - target_ref[...]
    copies_ref[...] = jnp.broadcast_to(residual[None], copies_ref.shape)


def settle(parts, target):
    return pl.pallas_call(
        settle_kernel,
        in_specs=[whole(), whole()],
        out_specs=whole(),
        out_shape=shape(parts.shape),
        compiler_params=params(),
        cost_estimate=cost(2 * parts.size, 8 * parts.size),
    )(parts, target)


def far_terms_kernel(own_ref, other_ref, high_ref, low_ref, sums_ref):
    columns, width = own_ref.shape[1], sums_ref.shape[1]
    lines = []
    for core, ref in enumerate((own_ref, other_ref)):
        tile = swapped(ref[...]) if core else ref[...]
        for term, out in zip(cut(tile, 2), (high_ref, low_ref)):
            out[:, core * columns : (core + 1) * columns] = term
        part = jnp.sum(tile, axis=0, keepdims=True)
        lines += [part[:, place : place + width] for place in range(0, columns, width)]
    lines.append(jnp.zeros((rider - len(lines), width), jnp.float32))
    sums_ref[...] = jnp.concatenate(lines, axis=0)


def far_terms(own, other, half):
    rows, columns = own.shape
    return pl.pallas_call(
        far_terms_kernel,
        in_specs=[whole(), whole()],
        out_specs=[whole()] * 3,
        out_shape=[shape((rows, 2 * columns), jnp.bfloat16)] * 2 + [shape((rider, half))],
        compiler_params=params(),
        cost_estimate=cost(8 * own.size, 16 * own.size),
    )(own, other)


def gradient_kernel(place_ref, own_ref, other_ref, residual_ref, sums_ref, out_ref):
    count, rows, half = residual_ref.shape
    rows = rows // 2
    places = [count - 1 - place for place in ring_places(place_ref, count)]
    residual = from_ring(residual_ref, places, rows)
    own = mul_terms(cut(own_ref[...], 2), cut(residual, 2), 0, 0)
    other = mul_terms(cut(other_ref[...], 2), cut(swapped(residual), 2), 0, 0)
    last = out_ref.shape[0] - 1
    for step in range(last + 1):
        block = slice(step * rows, (step + 1) * rows)
        out_ref[last - step, :rows] = own[block]
        out_ref[last - step, rows : 2 * rows] = other[block]
    out_ref[:, 2 * rows :] = jnp.broadcast_to(sums_ref[...][None], (last + 1, rider, half))


def gradient(place, tiles, residual, sums):
    _, rows, half = residual.shape
    count = 2 * tiles[0].shape[1] // rows
    return pl.pallas_call(
        gradient_kernel,
        in_specs=[whole(pltpu.SMEM)] + [whole()] * 4,
        out_specs=whole(),
        out_shape=shape((count, rows + rider, half)),
        compiler_params=params(),
        cost_estimate=cost(12 * tiles[0].size * half, 4 * 1024 * 1024),
    )(place, *tiles, residual, sums)


def collect_kernel(parts_ref, grad_ref, copies_ref, largest_ref):
    rows = grad_ref.shape[0]
    total = jnp.sum(parts_ref[...], axis=0)
    grad_ref[...] = total[:rows]
    copies_ref[...] = jnp.broadcast_to(total[None, :rows], copies_ref.shape)
    largest = jnp.max(jnp.max(total[rows:], axis=0, keepdims=True), axis=1, keepdims=True)
    largest_ref[...] = jnp.broadcast_to(largest, largest_ref.shape)


def collect(parts):
    count, packed, half = parts.shape
    rows = packed - rider
    return pl.pallas_call(
        collect_kernel,
        in_specs=[whole()],
        out_specs=[whole()] * 3,
        out_shape=[
            shape((rows, half), jnp.float32),
            shape((count, rows, half), jnp.float32),
            shape((rider, half), jnp.float32),
        ],
        compiler_params=params(),
        cost_estimate=cost(2 * parts.size, 8 * parts.size),
    )(parts)


def product_kernel(place_ref, high_ref, low_ref, grad_ref, largest_ref, out_ref):
    rows = grad_ref.shape[1] // 2
    count, _, half = out_ref.shape
    grads = jnp.concatenate([flat(grad_ref[:, :rows]), flat(grad_ref[:, rows:])], axis=0)
    total = mul_terms([high_ref[...], low_ref[...]], cut(grads, 2), 1, 0)
    to_ring(total, out_ref, ring_places(place_ref, count), rows)
    out_ref[:, 2 * rows :] = jnp.broadcast_to(largest_ref[...][None], (count, rider, half))


def product(place, terms, grads, largest):
    _, rows, half = grads.shape
    count = terms[0].shape[0] // rows
    return pl.pallas_call(
        product_kernel,
        in_specs=[whole(pltpu.SMEM)] + [whole()] * 4,
        out_specs=whole(),
        out_shape=shape((count, rows + rider, half)),
        compiler_params=params(),
        cost_estimate=cost(6 * terms[0].size * half, 4 * 1024 * 1024),
    )(place, *terms, grads, largest)


def finish_kernel(scale, parts_ref, grad_ref, theta_ref):
    rows = grad_ref.shape[0]
    total = jnp.sum(parts_ref[:, :rows], axis=0)
    largest = jnp.max(parts_ref[:, rows:], axis=0)
    largest = jnp.max(jnp.max(largest, axis=0, keepdims=True), axis=1, keepdims=True)
    step_size = 1.0 / largest
    theta_ref[...] = (2.0 * step_size * grad_ref[...] - step_size * step_size * total) * scale


def finish(parts, grad, scale):
    def body(*refs):
        finish_kernel(scale, *refs)

    return pl.pallas_call(
        body,
        in_specs=[whole(), whole()],
        out_specs=whole(),
        out_shape=shape(grad.shape),
        compiler_params=params(),
        cost_estimate=cost(2 * parts.size, 4 * parts.size),
    )(parts, grad)


def spread_kernel(core_ref, weight_ref, centre_ref, out_ref, packed_ref, semaphores):
    half, width = weight_ref.shape[1] // 2, packed_ref.shape[1]
    packed_ref[:, half : width - half] = centre_ref[...]
    first, second = weight_ref[:, :half], weight_ref[:, half:]
    low = core_ref[0] == 0
    packed_ref[:, :half] = jnp.where(low, second, first)
    packed_ref[:, width - half :] = jnp.where(low, first, second)
    moves = [
        pltpu.make_async_copy(packed_ref, out_ref.at[place], semaphores.at[place]) for place in range(out_ref.shape[0])
    ]
    for move in moves:
        move.start()
    for move in moves:
        move.wait()


def spread(weights, centres, count):
    rows, width = weights.shape[0], weights.shape[1] + centres.shape[1]
    return pl.pallas_call(
        spread_kernel,
        in_specs=[whole(pltpu.SMEM), whole(), whole()],
        out_specs=whole(pl.ANY),
        out_shape=shape((count, rows, width)),
        scratch_shapes=[pltpu.VMEM((rows, width), jnp.float32), pltpu.SemaphoreType.DMA((count,))],
        compiler_params=params(most_bytes),
        cost_estimate=cost(0, 4 * count * rows * width),
    )(lax.axis_index("core").reshape(1).astype(jnp.int32), weights, centres)


def assemble_kernel(count, *refs):
    for place, ref in enumerate(refs[:count]):
        rows = ref.shape[0] // 2
        for part, out_ref in enumerate(refs[count:]):
            out_ref[place * rows : (place + 1) * rows, :] = ref[part * rows : (part + 1) * rows, :]


def assemble(pieces):
    count = len(pieces)
    rows, width = pieces[0].shape
    return pl.pallas_call(
        functools.partial(assemble_kernel, count),
        in_specs=[whole()] * count,
        out_specs=[whole()] * 2,
        out_shape=[shape((count * rows // 2, width))] * 2,
        compiler_params=params(),
        cost_estimate=cost(0, 8 * count * rows * width),
    )(*pieces)


def backward(copies, axis):
    order = [list(range(lax.axis_size(axis)))[::-1]]
    return lax.all_to_all(copies, axis, 0, 0, axis_index_groups=order)


def gather(value, axis):
    copies = jnp.broadcast_to(value[None], (lax.axis_size(axis),) + value.shape)
    return lax.all_to_all(copies, axis, 0, 0)


def ring_pieces(value):
    count, low = lax.axis_size(ring), lax.axis_size("z_lo")

    def slot(place):
        return place % low * (count // low) + place // low

    def hop(held, step):
        pairs = [(slot(place), slot((place + step) % count)) for place in range(count)]
        return lax.ppermute(held, ("z_lo", "z_hi"), pairs)

    ahead, behind = [value], [value]
    for step in range(1, count):
        if step % 2:
            behind.append(hop(behind[-1], 1))
        else:
            ahead.append(hop(ahead[-1], -1))
    return ahead + behind[:0:-1]


def from_other(value):
    return lax.ppermute(value, "core", swap)


def halves(rows):
    core = lax.axis_index("core")
    half = rows.shape[1] // 2
    first, second = rows[:, :half], rows[:, half:]
    return jnp.where(core == 0, first, second), jnp.where(core == 0, second, first)


def to_rows(*columns):
    core = lax.axis_index("core")
    rows = columns[0].shape[0] // 2
    own = jnp.concatenate([value[:rows] for value in columns], axis=0)
    other = from_other(jnp.concatenate([value[rows:] for value in columns], axis=0))
    first = jnp.where(core == 0, own, other)
    second = jnp.where(core == 0, other, own)
    both = jnp.concatenate([first, second], axis=1)
    return tuple(both[place * rows : (place + 1) * rows] for place in range(len(columns)))


def shards(batch_features, centre_features, targets, weights):
    rows, width = targets.shape
    half = width // 2
    total_rows = rows * lax.axis_size(plane) * lax.axis_size(ring) * 2
    place = lax.axis_index(ring)

    place = place.reshape(1).astype(jnp.int32)

    centres = spread(weights, centre_features, lax.axis_size(plane))
    centres = backward(centres, plane)
    pieces = ring_pieces(jnp.concatenate([batch_features, centre_features], axis=0))
    batch, far = assemble(pieces)
    batch_other = from_other(batch)
    far_other = from_other(far)
    tile, theirs, mine = tile_of(batch, batch_other, centres, half, 2)
    pred = join(place, mine, from_other(theirs), rows)
    tiles = tile, from_other(tile)
    target_mine, target_theirs = halves(targets)
    target = jnp.concatenate([target_mine, from_other(target_theirs)], axis=0)
    parts = lax.all_to_all(pred, ring, 0, 0)
    residuals = settle(parts, target)
    residual_full = backward(residuals, ring)

    (far_tile,) = tile_of(far, far_other, centres, half)
    *fars, sums = far_terms(far_tile, from_other(far_tile), half)
    parts = lax.all_to_all(gradient(place, tiles, residual_full, sums), plane, 0, 0)
    grad, copies, largest = collect(parts)
    grad_full = backward(copies, plane)
    parts = lax.all_to_all(product(place, fars, grad_full, largest), ring, 0, 0)
    theta = finish(parts, grad, total_rows / math.sqrt(total_rows))
    return to_rows(residuals[0], theta)


def solution(mesh):
    fine = Mesh(
        mesh.devices.reshape(4, 4, 4, 2, 2),
        ("x", "z_lo", "y", "z_hi", "core"),
    )
    by_batch = P(("x", "z_lo", "y", "z_hi", "core"), None)
    by_centre = P(("y", "z_hi", "core", "x", "z_lo"), None)
    return jax.shard_map(
        shards,
        mesh=fine,
        in_specs=(by_batch, by_centre, by_batch, by_centre),
        out_specs=(by_batch, by_centre),
        check_vma=False,
    )
```

```python
import functools
import math

import jax
import jax.numpy as jnp
from jax import lax
from jax.experimental import pallas as pl
from jax.experimental.pallas import tpu as pltpu
from jax.sharding import Mesh
from jax.sharding import PartitionSpec as P

length_scale = 0.5
softening = 0.01
plane = ("x", "y")
ring = ("z_hi", "z_lo")
swap = [(0, 1), (1, 0)]
ring_low = 4
ring_order = ("z_lo", "z_hi")
rider = 8
vmem_bytes = 24 * 1024 * 1024
most_bytes = 60 * 1024 * 1024


def whole(space=pltpu.VMEM):
    return pl.BlockSpec(memory_space=space)


def params(size=vmem_bytes):
    return pltpu.CompilerParams(vmem_limit_bytes=size)


def shape(sizes, dtype=jnp.float32):
    return jax.ShapeDtypeStruct(sizes, dtype)


def cost(flops, moved, transcendentals=0):
    return pl.CostEstimate(flops=flops, bytes_accessed=moved, transcendentals=transcendentals)


def dot(left, right, left_dim, right_dim):
    return lax.dot_general(
        left,
        right,
        (((left_dim,), (right_dim,)), ((), ())),
        precision=lax.Precision.HIGHEST,
        preferred_element_type=jnp.float32,
    )


def flat(value):
    return value.reshape(-1, value.shape[-1])


def high(value):
    return value.astype(jnp.bfloat16)


def cut(value, count):
    terms = []
    for _ in range(count):
        terms.append(high(value))
        value = value - terms[-1].astype(jnp.float32)
    return terms


def mul(left, right, left_dim, right_dim):
    return lax.dot_general(
        left, right, (((left_dim,), (right_dim,)), ((), ())), preferred_element_type=jnp.float32
    )


def mul_terms(left, right, left_dim, right_dim):
    count = len(left)
    total = None
    for order in reversed(range(count)):
        for place in range(order + 1):
            term = mul(left[place], right[order - place], left_dim, right_dim)
            total = term if total is None else total + term
    return total


def tile_block(left, left_norms, right_refs, norm_ref, columns):
    inner = mul_terms(left, [ref[columns, :] for ref in right_refs], 1, 1)
    squared = left_norms + norm_ref[:1, columns] - 2.0 * inner
    return jnp.exp(-jnp.sqrt(squared + softening) / length_scale)


def square_sums(rows):
    return jnp.sum(rows * rows, axis=1, keepdims=True)


def tile_kernel(half, shared, own_ref, other_ref, packed_ref, *refs):
    outs, refs = refs[: 1 + shared], refs[1 + shared :]
    left_ref, right_refs, rights, norm_ref, tile_ref, come, leave = refs[0], refs[1:3], refs[3:6], *refs[6:10]
    count, each, width = packed_ref.shape
    rows, depth = own_ref.shape
    step = count // 2
    centre_ref = packed_ref.at[:, :, pl.ds(half, depth)]
    pairs = [
        (centre_ref.at[pl.ds(0, step)], right_refs[0]),
        (own_ref, left_ref.at[pl.ds(0, rows)]),
        (other_ref, left_ref.at[pl.ds(rows, rows)]),
        (centre_ref.at[pl.ds(step, step)], right_refs[1]),
    ]
    if shared:
        weight_refs, share_refs = refs[10:12], refs[12:14]
        for place, columns in enumerate((pl.ds(0, half), pl.ds(width - half, half))):
            pairs.append((packed_ref.at[:, :, columns], weight_refs[place]))
    moves = [pltpu.make_async_copy(*pair, come.at[place]) for place, pair in enumerate(pairs)]
    for move in moves:
        move.start()
    shares, gone = [None] * shared, []

    def send(source, target):
        gone.append(pltpu.make_async_copy(source, target, leave.at[len(gone)]))
        gone[-1].start()

    for place, move in ((0, moves[0]), (1, moves[3])):
        columns = pl.ds(place * step * each, step * each)
        move.wait()
        right = flat(right_refs[place][...])
        for term, ref in zip(cut(right, 3), rights):
            ref[columns, :] = term
        ones = jnp.ones((8, depth), jnp.float32)
        norm_ref[:, columns] = dot(ones, right * right, 1, 1)
        if place == 0:
            moves[1].wait()
            moves[2].wait()
            left = left_ref[...]
            left_norms = square_sums(left)
            left = cut(left, 3)
        block = tile_block(left, left_norms, rights, norm_ref, columns)
        tile_ref[:, columns] = block
        send(tile_ref.at[:, columns], outs[0].at[:, columns])
        if shared:
            if place == 0:
                moves[4].wait()
                moves[5].wait()
            terms = cut(block, 2)
            for part, ref in enumerate(weight_refs):
                weights = cut(flat(ref[place * step : (place + 1) * step]), 2)
                share = mul_terms(terms, weights, 1, 0)
                shares[part] = share if shares[part] is None else shares[part] + share
    for part in range(shared):
        share_refs[part][...] = shares[part]
        send(share_refs[part], outs[1 + part])
    for move in gone:
        move.wait()


def tile_of(own, other, packed, half, shared=0):
    count, each, _ = packed.shape
    rows, depth = own.shape
    rows, columns = 2 * rows, count * each
    scratch = [pltpu.VMEM((rows, depth), jnp.float32)]
    scratch += [pltpu.VMEM((count // 2, each, depth), jnp.float32)] * 2
    scratch += [pltpu.VMEM((columns, depth), jnp.bfloat16)] * 3
    scratch += [pltpu.VMEM((8, columns), jnp.float32), pltpu.VMEM((rows, columns), jnp.float32)]
    scratch += [pltpu.SemaphoreType.DMA((4 + shared,)), pltpu.SemaphoreType.DMA((2 + shared,))]
    scratch += [pltpu.VMEM((count, each, half), jnp.float32)] * shared
    scratch += [pltpu.VMEM((rows, half), jnp.float32)] * shared
    return pl.pallas_call(
        functools.partial(tile_kernel, half, shared),
        in_specs=[whole(pl.ANY)] * 3,
        out_specs=[whole(pl.ANY)] * (1 + shared),
        out_shape=[shape((rows, columns))] + [shape((rows, half))] * shared,
        scratch_shapes=scratch,
        compiler_params=params(most_bytes),
        cost_estimate=cost(12 * rows * columns * depth, 6 * 1024 * 1024, 2 * rows * columns),
    )(own, other, packed)


def swapped(rows):
    half = rows.shape[0] // 2
    return jnp.concatenate([rows[half:], rows[:half]], axis=0)


def ring_places(place_ref, count):
    places = [lax.rem(place_ref[0] + step, count) for step in range(count)]
    return [lax.rem(place, ring_low) * (count // ring_low) + lax.div(place, ring_low) for place in places]


def from_ring(ref, places, rows):
    mine = [ref[place, :rows] for place in places]
    return jnp.concatenate(mine + [ref[place, rows : 2 * rows] for place in places], axis=0)


def to_ring(total, ref, places, rows):
    middle = total.shape[0] // 2
    for step, place in enumerate(places):
        ref[place, :rows] = total[step * rows : (step + 1) * rows]
        ref[place, rows : 2 * rows] = total[middle + step * rows : middle + (step + 1) * rows]


def join_kernel(place_ref, own_ref, other_ref, pred_ref):
    count, rows, _ = pred_ref.shape
    to_ring(own_ref[...] + swapped(other_ref[...]), pred_ref, ring_places(place_ref, count), rows // 2)


def join(place, own, other, rows):
    count, half = own.shape
    return pl.pallas_call(
        join_kernel,
        in_specs=[whole(pltpu.SMEM), whole(), whole()],
        out_specs=whole(),
        out_shape=shape((count // (2 * rows), 2 * rows, half)),
        compiler_params=params(),
        cost_estimate=cost(own.size, 12 * own.size),
    )(place, own, other)


def settle_kernel(parts_ref, target_ref, copies_ref):
    residual = jnp.sum(parts_ref[...], axis=0) - target_ref[...]
    copies_ref[...] = jnp.broadcast_to(residual[None], copies_ref.shape)


def settle(parts, target):
    return pl.pallas_call(
        settle_kernel,
        in_specs=[whole(), whole()],
        out_specs=whole(),
        out_shape=shape(parts.shape),
        compiler_params=params(),
        cost_estimate=cost(2 * parts.size, 8 * parts.size),
    )(parts, target)


def far_terms_kernel(own_ref, other_ref, high_ref, low_ref, sums_ref):
    columns, width = own_ref.shape[1], sums_ref.shape[1]
    lines = []
    for core, ref in enumerate((own_ref, other_ref)):
        tile = swapped(ref[...]) if core else ref[...]
        for term, out in zip(cut(tile, 2), (high_ref, low_ref)):
            out[:, core * columns : (core + 1) * columns] = term
        part = jnp.sum(tile, axis=0, keepdims=True)
        lines += [part[:, place : place + width] for place in range(0, columns, width)]
    lines.append(jnp.zeros((rider - len(lines), width), jnp.float32))
    sums_ref[...] = jnp.concatenate(lines, axis=0)


def far_terms(own, other, half):
    rows, columns = own.shape
    return pl.pallas_call(
        far_terms_kernel,
        in_specs=[whole(), whole()],
        out_specs=[whole()] * 3,
        out_shape=[shape((rows, 2 * columns), jnp.bfloat16)] * 2 + [shape((rider, half))],
        compiler_params=params(),
        cost_estimate=cost(8 * own.size, 16 * own.size),
    )(own, other)


def gradient_kernel(place_ref, own_ref, other_ref, residual_ref, sums_ref, out_ref):
    count, rows, half = residual_ref.shape
    rows = rows // 2
    places = [count - 1 - place for place in ring_places(place_ref, count)]
    residual = from_ring(residual_ref, places, rows)
    own = mul_terms(cut(own_ref[...], 2), cut(residual, 2), 0, 0)
    other = mul_terms(cut(other_ref[...], 2), cut(swapped(residual), 2), 0, 0)
    last = out_ref.shape[0] - 1
    for step in range(last + 1):
        block = slice(step * rows, (step + 1) * rows)
        out_ref[last - step, :rows] = own[block]
        out_ref[last - step, rows : 2 * rows] = other[block]
    out_ref[:, 2 * rows :] = jnp.broadcast_to(sums_ref[...][None], (last + 1, rider, half))


def gradient(place, tiles, residual, sums):
    _, rows, half = residual.shape
    count = 2 * tiles[0].shape[1] // rows
    return pl.pallas_call(
        gradient_kernel,
        in_specs=[whole(pltpu.SMEM)] + [whole()] * 4,
        out_specs=whole(),
        out_shape=shape((count, rows + rider, half)),
        compiler_params=params(),
        cost_estimate=cost(12 * tiles[0].size * half, 4 * 1024 * 1024),
    )(place, *tiles, residual, sums)


def collect_kernel(parts_ref, grad_ref, copies_ref, largest_ref):
    rows = grad_ref.shape[0]
    total = jnp.sum(parts_ref[...], axis=0)
    grad_ref[...] = total[:rows]
    copies_ref[...] = jnp.broadcast_to(total[None, :rows], copies_ref.shape)
    largest = jnp.max(jnp.max(total[rows:], axis=0, keepdims=True), axis=1, keepdims=True)
    largest_ref[...] = jnp.broadcast_to(largest, largest_ref.shape)


def collect(parts):
    count, packed, half = parts.shape
    rows = packed - rider
    return pl.pallas_call(
        collect_kernel,
        in_specs=[whole()],
        out_specs=[whole()] * 3,
        out_shape=[
            shape((rows, half), jnp.float32),
            shape((count, rows, half), jnp.float32),
            shape((rider, half), jnp.float32),
        ],
        compiler_params=params(),
        cost_estimate=cost(2 * parts.size, 8 * parts.size),
    )(parts)


def product_kernel(place_ref, high_ref, low_ref, grad_ref, largest_ref, out_ref):
    rows = grad_ref.shape[1] // 2
    count, _, half = out_ref.shape
    grads = jnp.concatenate([flat(grad_ref[:, :rows]), flat(grad_ref[:, rows:])], axis=0)
    total = mul_terms([high_ref[...], low_ref[...]], cut(grads, 2), 1, 0)
    places = [count - 1 - place for place in ring_places(place_ref, count)]
    to_ring(total, out_ref, places, rows)
    out_ref[:, 2 * rows :] = jnp.broadcast_to(largest_ref[...][None], (count, rider, half))


def product(place, terms, grads, largest):
    _, rows, half = grads.shape
    count = terms[0].shape[0] // rows
    return pl.pallas_call(
        product_kernel,
        in_specs=[whole(pltpu.SMEM)] + [whole()] * 4,
        out_specs=whole(),
        out_shape=shape((count, rows + rider, half)),
        compiler_params=params(),
        cost_estimate=cost(6 * terms[0].size * half, 4 * 1024 * 1024),
    )(place, *terms, grads, largest)


def finish_kernel(scale, parts_ref, grad_ref, theta_ref):
    rows = grad_ref.shape[0]
    total = jnp.sum(parts_ref[:, :rows], axis=0)
    largest = jnp.max(parts_ref[:, rows:], axis=0)
    largest = jnp.max(jnp.max(largest, axis=0, keepdims=True), axis=1, keepdims=True)
    step_size = 1.0 / largest
    theta_ref[...] = (2.0 * step_size * grad_ref[...] - step_size * step_size * total) * scale


def finish(parts, grad, scale):
    def body(*refs):
        finish_kernel(scale, *refs)

    return pl.pallas_call(
        body,
        in_specs=[whole(), whole()],
        out_specs=whole(),
        out_shape=shape(grad.shape),
        compiler_params=params(),
        cost_estimate=cost(2 * parts.size, 4 * parts.size),
    )(parts, grad)


def spread_kernel(core_ref, weight_ref, centre_ref, out_ref, packed_ref, semaphores):
    half, width = weight_ref.shape[1] // 2, packed_ref.shape[1]
    packed_ref[:, half : width - half] = centre_ref[...]
    first, second = weight_ref[:, :half], weight_ref[:, half:]
    low = core_ref[0] == 0
    packed_ref[:, :half] = jnp.where(low, second, first)
    packed_ref[:, width - half :] = jnp.where(low, first, second)
    moves = [
        pltpu.make_async_copy(packed_ref, out_ref.at[place], semaphores.at[place]) for place in range(out_ref.shape[0])
    ]
    for move in moves:
        move.start()
    for move in moves:
        move.wait()


def spread(weights, centres, count):
    rows, width = weights.shape[0], weights.shape[1] + centres.shape[1]
    return pl.pallas_call(
        spread_kernel,
        in_specs=[whole(pltpu.SMEM), whole(), whole()],
        out_specs=whole(pl.ANY),
        out_shape=shape((count, rows, width)),
        scratch_shapes=[pltpu.VMEM((rows, width), jnp.float32), pltpu.SemaphoreType.DMA((count,))],
        compiler_params=params(most_bytes),
        cost_estimate=cost(0, 4 * count * rows * width),
    )(lax.axis_index("core").reshape(1).astype(jnp.int32), weights, centres)


def assemble_kernel(count, *refs):
    for place, ref in enumerate(refs[:count]):
        rows = ref.shape[0] // 2
        for part, out_ref in enumerate(refs[count:]):
            out_ref[place * rows : (place + 1) * rows, :] = ref[part * rows : (part + 1) * rows, :]


def assemble(pieces):
    count = len(pieces)
    rows, width = pieces[0].shape
    return pl.pallas_call(
        functools.partial(assemble_kernel, count),
        in_specs=[whole()] * count,
        out_specs=[whole()] * 2,
        out_shape=[shape((count * rows // 2, width))] * 2,
        compiler_params=params(),
        cost_estimate=cost(0, 8 * count * rows * width),
    )(*pieces)


def backward(copies, axis):
    order = [list(range(lax.axis_size(axis)))[::-1]]
    return lax.all_to_all(copies, axis, 0, 0, axis_index_groups=order)


def gather(value, axis):
    copies = jnp.broadcast_to(value[None], (lax.axis_size(axis),) + value.shape)
    return lax.all_to_all(copies, axis, 0, 0)


def ring_pieces(value):
    count, low = lax.axis_size(ring), lax.axis_size("z_lo")

    def slot(place):
        return place % low * (count // low) + place // low

    def hop(held, step):
        pairs = [(slot(place), slot((place + step) % count)) for place in range(count)]
        return lax.ppermute(held, ("z_lo", "z_hi"), pairs)

    ahead, behind = [value], [value]
    for step in range(1, count):
        if step % 2:
            behind.append(hop(behind[-1], 1))
        else:
            ahead.append(hop(ahead[-1], -1))
    return ahead + behind[:0:-1]


def from_other(value):
    return lax.ppermute(value, "core", swap)


def halves(rows):
    core = lax.axis_index("core")
    half = rows.shape[1] // 2
    first, second = rows[:, :half], rows[:, half:]
    return jnp.where(core == 0, first, second), jnp.where(core == 0, second, first)


def to_rows(*columns):
    core = lax.axis_index("core")
    rows = columns[0].shape[0] // 2
    own = jnp.concatenate([value[:rows] for value in columns], axis=0)
    other = from_other(jnp.concatenate([value[rows:] for value in columns], axis=0))
    first = jnp.where(core == 0, own, other)
    second = jnp.where(core == 0, other, own)
    both = jnp.concatenate([first, second], axis=1)
    return tuple(both[place * rows : (place + 1) * rows] for place in range(len(columns)))


def shards(batch_features, centre_features, targets, weights):
    rows, width = targets.shape
    half = width // 2
    total_rows = rows * lax.axis_size(plane) * lax.axis_size(ring) * 2
    place = lax.axis_index(ring)

    place = place.reshape(1).astype(jnp.int32)

    centres = spread(weights, centre_features, lax.axis_size(plane))
    centres = backward(centres, plane)
    pieces = ring_pieces(jnp.concatenate([batch_features, centre_features], axis=0))
    batch, far = assemble(pieces)
    batch_other = from_other(batch)
    far_other = from_other(far)
    tile, theirs, mine = tile_of(batch, batch_other, centres, half, 2)
    pred = join(place, mine, from_other(theirs), rows)
    tiles = tile, from_other(tile)
    target_mine, target_theirs = halves(targets)
    target = jnp.concatenate([target_mine, from_other(target_theirs)], axis=0)
    parts = lax.all_to_all(pred, ring_order, 0, 0)
    residuals = settle(parts, target)
    residual_full = backward(residuals, ring_order)

    (far_tile,) = tile_of(far, far_other, centres, half)
    *fars, sums = far_terms(far_tile, from_other(far_tile), half)
    parts = lax.all_to_all(gradient(place, tiles, residual_full, sums), plane, 0, 0)
    grad, copies, largest = collect(parts)
    grad_full = backward(copies, plane)
    parts = backward(product(place, fars, grad_full, largest), ring_order)
    theta = finish(parts, grad, total_rows / math.sqrt(total_rows))
    return to_rows(residuals[0], theta)


def solution(mesh):
    fine = Mesh(
        mesh.devices.reshape(4, 4, 4, 2, 2),
        ("x", "z_lo", "y", "z_hi", "core"),
    )
    by_batch = P(("x", "z_lo", "y", "z_hi", "core"), None)
    by_centre = P(("y", "z_hi", "core", "x", "z_lo"), None)
    return jax.shard_map(
        shards,
        mesh=fine,
        in_specs=(by_batch, by_centre, by_batch, by_centre),
        out_specs=(by_batch, by_centre),
        check_vma=False,
    )
```

```python
import functools
import math

import jax
import jax.numpy as jnp
from jax import lax
from jax.experimental import pallas as pl
from jax.experimental.pallas import tpu as pltpu
from jax.sharding import Mesh
from jax.sharding import PartitionSpec as P

length_scale = 0.5
softening = 0.01
plane = ("x", "y")
ring = ("z_hi", "z_lo")
swap = [(0, 1), (1, 0)]
ring_low = 4
ring_order = ("z_lo", "z_hi")
rider = 8
vmem_bytes = 24 * 1024 * 1024
most_bytes = 60 * 1024 * 1024


def whole(space=pltpu.VMEM):
    return pl.BlockSpec(memory_space=space)


def params(size=vmem_bytes):
    return pltpu.CompilerParams(vmem_limit_bytes=size)


def shape(sizes, dtype=jnp.float32):
    return jax.ShapeDtypeStruct(sizes, dtype)


def cost(flops, moved, transcendentals=0):
    return pl.CostEstimate(flops=flops, bytes_accessed=moved, transcendentals=transcendentals)


def dot(left, right, left_dim, right_dim):
    return lax.dot_general(
        left,
        right,
        (((left_dim,), (right_dim,)), ((), ())),
        precision=lax.Precision.HIGHEST,
        preferred_element_type=jnp.float32,
    )


def flat(value):
    return value.reshape(-1, value.shape[-1])


def high(value):
    return value.astype(jnp.bfloat16)


def cut(value, count):
    terms = []
    for _ in range(count):
        terms.append(high(value))
        value = value - terms[-1].astype(jnp.float32)
    return terms


def mul(left, right, left_dim, right_dim):
    return lax.dot_general(
        left, right, (((left_dim,), (right_dim,)), ((), ())), preferred_element_type=jnp.float32
    )


def mul_terms(left, right, left_dim, right_dim):
    count = len(left)
    total = None
    for order in reversed(range(count)):
        for place in range(order + 1):
            term = mul(left[place], right[order - place], left_dim, right_dim)
            total = term if total is None else total + term
    return total


def tile_block(left, left_norms, right_refs, norm_ref, columns):
    inner = mul_terms(left, [ref[columns, :] for ref in right_refs], 1, 1)
    squared = left_norms + norm_ref[:1, columns] - 2.0 * inner
    return jnp.exp(-jnp.sqrt(squared + softening) / length_scale)


def square_sums(rows):
    return jnp.sum(rows * rows, axis=1, keepdims=True)


def tile_kernel(half, shared, own_ref, other_ref, packed_ref, *refs):
    outs, refs = refs[: 1 + shared], refs[1 + shared :]
    left_ref, right_refs, rights, norm_ref, tile_ref, come, leave = refs[0], refs[1:3], refs[3:6], *refs[6:10]
    count, each, width = packed_ref.shape
    rows, depth = own_ref.shape
    step = count // 2
    centre_ref = packed_ref.at[:, :, pl.ds(half, depth)]
    pairs = [
        (centre_ref.at[pl.ds(0, step)], right_refs[0]),
        (own_ref, left_ref.at[pl.ds(0, rows)]),
        (other_ref, left_ref.at[pl.ds(rows, rows)]),
        (centre_ref.at[pl.ds(step, step)], right_refs[1]),
    ]
    if shared:
        weight_refs, share_refs = refs[10:12], refs[12:14]
        for place, columns in enumerate((pl.ds(0, half), pl.ds(width - half, half))):
            pairs.append((packed_ref.at[:, :, columns], weight_refs[place]))
    moves = [pltpu.make_async_copy(*pair, come.at[place]) for place, pair in enumerate(pairs)]
    for move in moves:
        move.start()
    shares, gone = [None] * shared, []

    def send(source, target):
        gone.append(pltpu.make_async_copy(source, target, leave.at[len(gone)]))
        gone[-1].start()

    for place, move in ((0, moves[0]), (1, moves[3])):
        columns = pl.ds(place * step * each, step * each)
        move.wait()
        right = flat(right_refs[place][...])
        for term, ref in zip(cut(right, 3), rights):
            ref[columns, :] = term
        ones = jnp.ones((8, depth), jnp.float32)
        norm_ref[:, columns] = dot(ones, right * right, 1, 1)
        if place == 0:
            moves[1].wait()
            moves[2].wait()
            left = left_ref[...]
            left_norms = square_sums(left)
            left = cut(left, 3)
        block = tile_block(left, left_norms, rights, norm_ref, columns)
        tile_ref[:, columns] = block
        send(tile_ref.at[:, columns], outs[0].at[:, columns])
        if shared:
            if place == 0:
                moves[4].wait()
                moves[5].wait()
            terms = cut(block, 2)
            for part, ref in enumerate(weight_refs):
                weights = cut(flat(ref[place * step : (place + 1) * step]), 2)
                share = mul_terms(terms, weights, 1, 0)
                shares[part] = share if shares[part] is None else shares[part] + share
    for part in range(shared):
        share_refs[part][...] = shares[part]
        send(share_refs[part], outs[1 + part])
    for move in gone:
        move.wait()


def tile_of(own, other, packed, half, shared=0):
    count, each, _ = packed.shape
    rows, depth = own.shape
    rows, columns = 2 * rows, count * each
    scratch = [pltpu.VMEM((rows, depth), jnp.float32)]
    scratch += [pltpu.VMEM((count // 2, each, depth), jnp.float32)] * 2
    scratch += [pltpu.VMEM((columns, depth), jnp.bfloat16)] * 3
    scratch += [pltpu.VMEM((8, columns), jnp.float32), pltpu.VMEM((rows, columns), jnp.float32)]
    scratch += [pltpu.SemaphoreType.DMA((4 + shared,)), pltpu.SemaphoreType.DMA((2 + shared,))]
    scratch += [pltpu.VMEM((count, each, half), jnp.float32)] * shared
    scratch += [pltpu.VMEM((rows, half), jnp.float32)] * shared
    return pl.pallas_call(
        functools.partial(tile_kernel, half, shared),
        in_specs=[whole(pl.ANY)] * 3,
        out_specs=[whole(pl.ANY)] * (1 + shared),
        out_shape=[shape((rows, columns))] + [shape((rows, half))] * shared,
        scratch_shapes=scratch,
        compiler_params=params(most_bytes),
        cost_estimate=cost(12 * rows * columns * depth, 6 * 1024 * 1024, 2 * rows * columns),
    )(own, other, packed)


def swapped(rows):
    half = rows.shape[0] // 2
    return jnp.concatenate([rows[half:], rows[:half]], axis=0)


def ring_places(place_ref, count):
    places = [lax.rem(place_ref[0] + step, count) for step in range(count)]
    return [lax.rem(place, ring_low) * (count // ring_low) + lax.div(place, ring_low) for place in places]


def from_ring(ref, places, rows):
    mine = [ref[place, :rows] for place in places]
    return jnp.concatenate(mine + [ref[place, rows : 2 * rows] for place in places], axis=0)


def to_ring(total, ref, places, rows):
    middle = total.shape[0] // 2
    for step, place in enumerate(places):
        ref[place, :rows] = total[step * rows : (step + 1) * rows]
        ref[place, rows : 2 * rows] = total[middle + step * rows : middle + (step + 1) * rows]


def join_kernel(place_ref, own_ref, other_ref, pred_ref):
    count, rows, _ = pred_ref.shape
    to_ring(own_ref[...] + swapped(other_ref[...]), pred_ref, ring_places(place_ref, count), rows // 2)


def join(place, own, other, rows):
    count, half = own.shape
    return pl.pallas_call(
        join_kernel,
        in_specs=[whole(pltpu.SMEM), whole(), whole()],
        out_specs=whole(),
        out_shape=shape((count // (2 * rows), 2 * rows, half)),
        compiler_params=params(),
        cost_estimate=cost(own.size, 12 * own.size),
    )(place, own, other)


def settle_kernel(parts_ref, target_ref, copies_ref):
    residual = jnp.sum(parts_ref[...], axis=0) - target_ref[...]
    copies_ref[...] = jnp.broadcast_to(residual[None], copies_ref.shape)


def settle(parts, target):
    return pl.pallas_call(
        settle_kernel,
        in_specs=[whole(), whole()],
        out_specs=whole(),
        out_shape=shape(parts.shape),
        compiler_params=params(),
        cost_estimate=cost(2 * parts.size, 8 * parts.size),
    )(parts, target)


def far_terms_kernel(own_ref, other_ref, high_ref, low_ref, sums_ref):
    columns, width = own_ref.shape[1], sums_ref.shape[1]
    lines = []
    for core, ref in enumerate((own_ref, other_ref)):
        tile = swapped(ref[...]) if core else ref[...]
        for term, out in zip(cut(tile, 2), (high_ref, low_ref)):
            out[:, core * columns : (core + 1) * columns] = term
        part = jnp.sum(tile, axis=0, keepdims=True)
        lines += [part[:, place : place + width] for place in range(0, columns, width)]
    lines.append(jnp.zeros((rider - len(lines), width), jnp.float32))
    sums_ref[...] = jnp.concatenate(lines, axis=0)


def far_terms(own, other, half):
    rows, columns = own.shape
    return pl.pallas_call(
        far_terms_kernel,
        in_specs=[whole(), whole()],
        out_specs=[whole()] * 3,
        out_shape=[shape((rows, 2 * columns), jnp.bfloat16)] * 2 + [shape((rider, half))],
        compiler_params=params(),
        cost_estimate=cost(8 * own.size, 16 * own.size),
    )(own, other)


def gradient_kernel(place_ref, own_ref, other_ref, residual_ref, sums_ref, out_ref):
    count, rows, half = residual_ref.shape
    rows = rows // 2
    places = [count - 1 - place for place in ring_places(place_ref, count)]
    residual = from_ring(residual_ref, places, rows)
    own = mul_terms(cut(own_ref[...], 2), cut(residual, 2), 0, 0)
    other = mul_terms(cut(other_ref[...], 2), cut(swapped(residual), 2), 0, 0)
    last = out_ref.shape[0] - 1
    for step in range(last + 1):
        block = slice(step * rows, (step + 1) * rows)
        out_ref[last - step, :rows] = own[block]
        out_ref[last - step, rows : 2 * rows] = other[block]
    out_ref[:, 2 * rows :] = jnp.broadcast_to(sums_ref[...][None], (last + 1, rider, half))


def gradient(place, tiles, residual, sums):
    _, rows, half = residual.shape
    count = 2 * tiles[0].shape[1] // rows
    return pl.pallas_call(
        gradient_kernel,
        in_specs=[whole(pltpu.SMEM)] + [whole()] * 4,
        out_specs=whole(),
        out_shape=shape((count, rows + rider, half)),
        compiler_params=params(),
        cost_estimate=cost(12 * tiles[0].size * half, 4 * 1024 * 1024),
    )(place, *tiles, residual, sums)


def collect_kernel(parts_ref, grad_ref, copies_ref, largest_ref):
    rows = grad_ref.shape[0]
    total = jnp.sum(parts_ref[...], axis=0)
    grad_ref[...] = total[:rows]
    copies_ref[...] = jnp.broadcast_to(total[None, :rows], copies_ref.shape)
    largest = jnp.max(jnp.max(total[rows:], axis=0, keepdims=True), axis=1, keepdims=True)
    largest_ref[...] = jnp.broadcast_to(largest, largest_ref.shape)


def collect(parts):
    count, packed, half = parts.shape
    rows = packed - rider
    return pl.pallas_call(
        collect_kernel,
        in_specs=[whole()],
        out_specs=[whole()] * 3,
        out_shape=[
            shape((rows, half), jnp.float32),
            shape((count, rows, half), jnp.float32),
            shape((rider, half), jnp.float32),
        ],
        compiler_params=params(),
        cost_estimate=cost(2 * parts.size, 8 * parts.size),
    )(parts)


def product_kernel(place_ref, high_ref, low_ref, grad_ref, largest_ref, out_ref):
    rows = grad_ref.shape[1] // 2
    count, _, half = out_ref.shape
    grads = jnp.concatenate([flat(grad_ref[:, :rows]), flat(grad_ref[:, rows:])], axis=0)
    total = mul_terms([high_ref[...], low_ref[...]], cut(grads, 2), 1, 0)
    places = [count - 1 - place for place in ring_places(place_ref, count)]
    to_ring(total, out_ref, places, rows)
    out_ref[:, 2 * rows :] = jnp.broadcast_to(largest_ref[...][None], (count, rider, half))


def product(place, terms, grads, largest):
    _, rows, half = grads.shape
    count = terms[0].shape[0] // rows
    return pl.pallas_call(
        product_kernel,
        in_specs=[whole(pltpu.SMEM)] + [whole()] * 4,
        out_specs=whole(),
        out_shape=shape((count, rows + rider, half)),
        compiler_params=params(),
        cost_estimate=cost(6 * terms[0].size * half, 4 * 1024 * 1024),
    )(place, *terms, grads, largest)


def finish_kernel(scale, parts_ref, grad_ref, theta_ref):
    rows = grad_ref.shape[0]
    total = jnp.sum(parts_ref[:, :rows], axis=0)
    largest = jnp.max(parts_ref[:, rows:], axis=0)
    largest = jnp.max(jnp.max(largest, axis=0, keepdims=True), axis=1, keepdims=True)
    step_size = 1.0 / largest
    theta_ref[...] = (2.0 * step_size * grad_ref[...] - step_size * step_size * total) * scale


def finish(parts, grad, scale):
    def body(*refs):
        finish_kernel(scale, *refs)

    return pl.pallas_call(
        body,
        in_specs=[whole(), whole()],
        out_specs=whole(),
        out_shape=shape(grad.shape),
        compiler_params=params(),
        cost_estimate=cost(2 * parts.size, 4 * parts.size),
    )(parts, grad)


def spread_kernel(core_ref, weight_ref, centre_ref, out_ref, packed_ref, semaphores):
    half, width = weight_ref.shape[1] // 2, packed_ref.shape[1]
    packed_ref[:, half : width - half] = centre_ref[...]
    first, second = weight_ref[:, :half], weight_ref[:, half:]
    low = core_ref[0] == 0
    packed_ref[:, :half] = jnp.where(low, second, first)
    packed_ref[:, width - half :] = jnp.where(low, first, second)
    moves = [
        pltpu.make_async_copy(packed_ref, out_ref.at[place], semaphores.at[place]) for place in range(out_ref.shape[0])
    ]
    for move in moves:
        move.start()
    for move in moves:
        move.wait()


def spread(weights, centres, count):
    rows, width = weights.shape[0], weights.shape[1] + centres.shape[1]
    return pl.pallas_call(
        spread_kernel,
        in_specs=[whole(pltpu.SMEM), whole(), whole()],
        out_specs=whole(pl.ANY),
        out_shape=shape((count, rows, width)),
        scratch_shapes=[pltpu.VMEM((rows, width), jnp.float32), pltpu.SemaphoreType.DMA((count,))],
        compiler_params=params(most_bytes),
        cost_estimate=cost(0, 4 * count * rows * width),
    )(lax.axis_index("core").reshape(1).astype(jnp.int32), weights, centres)


def assemble_kernel(count, *refs):
    for place, ref in enumerate(refs[:count]):
        rows = ref.shape[0] // 2
        for part, out_ref in enumerate(refs[count:]):
            out_ref[place * rows : (place + 1) * rows, :] = ref[part * rows : (part + 1) * rows, :]


def assemble(pieces):
    count = len(pieces)
    rows, width = pieces[0].shape
    return pl.pallas_call(
        functools.partial(assemble_kernel, count),
        in_specs=[whole()] * count,
        out_specs=[whole()] * 2,
        out_shape=[shape((count * rows // 2, width))] * 2,
        compiler_params=params(),
        cost_estimate=cost(0, 8 * count * rows * width),
    )(*pieces)


def served(axis):
    count = lax.axis_size(axis)
    if axis != plane:
        return list(range(count))
    side = lax.axis_size("y")
    return [(place // side + place) % side * side + place % side for place in range(count)]


def forward(parts, axis):
    return lax.all_to_all(parts, axis, 0, 0, axis_index_groups=[served(axis)])


def backward(copies, axis):
    order = [served(axis)[::-1]]
    return lax.all_to_all(copies, axis, 0, 0, axis_index_groups=order)


def gather(value, axis):
    copies = jnp.broadcast_to(value[None], (lax.axis_size(axis),) + value.shape)
    return lax.all_to_all(copies, axis, 0, 0)


def ring_pieces(value):
    count, low = lax.axis_size(ring), lax.axis_size("z_lo")

    def slot(place):
        return place % low * (count // low) + place // low

    def hop(held, step):
        pairs = [(slot(place), slot((place + step) % count)) for place in range(count)]
        return lax.ppermute(held, ("z_lo", "z_hi"), pairs)

    ahead, behind = [value], [value]
    for step in range(1, count):
        if step % 2:
            behind.append(hop(behind[-1], 1))
        else:
            ahead.append(hop(ahead[-1], -1))
    return ahead + behind[:0:-1]


def from_other(value):
    return lax.ppermute(value, "core", swap)


def halves(rows):
    core = lax.axis_index("core")
    half = rows.shape[1] // 2
    first, second = rows[:, :half], rows[:, half:]
    return jnp.where(core == 0, first, second), jnp.where(core == 0, second, first)


def to_rows(*columns):
    core = lax.axis_index("core")
    rows = columns[0].shape[0] // 2
    own = jnp.concatenate([value[:rows] for value in columns], axis=0)
    other = from_other(jnp.concatenate([value[rows:] for value in columns], axis=0))
    first = jnp.where(core == 0, own, other)
    second = jnp.where(core == 0, other, own)
    both = jnp.concatenate([first, second], axis=1)
    return tuple(both[place * rows : (place + 1) * rows] for place in range(len(columns)))


def shards(batch_features, centre_features, targets, weights):
    rows, width = targets.shape
    half = width // 2
    total_rows = rows * lax.axis_size(plane) * lax.axis_size(ring) * 2
    place = lax.axis_index(ring)

    place = place.reshape(1).astype(jnp.int32)

    centres = spread(weights, centre_features, lax.axis_size(plane))
    centres = backward(centres, plane)
    pieces = ring_pieces(jnp.concatenate([batch_features, centre_features], axis=0))
    batch, far = assemble(pieces)
    batch_other = from_other(batch)
    far_other = from_other(far)
    tile, theirs, mine = tile_of(batch, batch_other, centres, half, 2)
    pred = join(place, mine, from_other(theirs), rows)
    tiles = tile, from_other(tile)
    target_mine, target_theirs = halves(targets)
    target = jnp.concatenate([target_mine, from_other(target_theirs)], axis=0)
    parts = lax.all_to_all(pred, ring_order, 0, 0)
    residuals = settle(parts, target)
    residual_full = backward(residuals, ring_order)

    (far_tile,) = tile_of(far, far_other, centres, half)
    *fars, sums = far_terms(far_tile, from_other(far_tile), half)
    parts = forward(gradient(place, tiles, residual_full, sums), plane)
    grad, copies, largest = collect(parts)
    grad_full = backward(copies, plane)
    parts = backward(product(place, fars, grad_full, largest), ring_order)
    theta = finish(parts, grad, total_rows / math.sqrt(total_rows))
    return to_rows(residuals[0], theta)


def solution(mesh):
    fine = Mesh(
        mesh.devices.reshape(4, 4, 4, 2, 2),
        ("x", "z_lo", "y", "z_hi", "core"),
    )
    by_batch = P(("x", "z_lo", "y", "z_hi", "core"), None)
    by_centre = P(("y", "z_hi", "core", "x", "z_lo"), None)
    return jax.shard_map(
        shards,
        mesh=fine,
        in_specs=(by_batch, by_centre, by_batch, by_centre),
        out_specs=(by_batch, by_centre),
        check_vma=False,
    )
```
